512 devices in a mesh: rep: 64 (over y_hi, z, core), shard: 8 (over x, y_lo).
Axes of the slice: x: 4, y: 4 (y_hi: 2, y_lo: 2; y = y_hi * 2 + y_lo), z: 16, core: 2. Of those that a mesh axis runs over, the one named last changes fastest.
Arguments:
- gradients: bfloat16 [64, 32, 128, 128], P('rep', 'shard'), may hold values from -6 to 6
- momentum: float32 [64, 32, 128, 128], P('rep', 'shard'), may hold values from -12 to 12
- params: bfloat16 [32, 128, 128], P('shard'), may hold values from -3 to 3
- band_offsets: int32 [32, 2], P('shard'), may hold values from 0 to 112
Outputs:
- new_momentum: float32 [64, 32, 128, 128], P('rep', 'shard')
- new_params: bfloat16 [32, 128, 128], replicated
The draws below stay inside these ranges and needn't reach their ends.
All inputs are finite; a program needn't handle non-finite values.
Results may differ from the reference program's by a relative error of at most 0.001.
Values may be sent and summed in bfloat16 or wider, within the bound.
No kernel may reach another device: no remote copies, remote signals or barrier semaphores. Data moves between devices by JAX's collectives and lax.ppermute only.
A program may use at most 64 MiB of HBM per device.

```python
import math
import jax
import jax.numpy as jnp
from jax import lax

TILE = 128
BAND = 16
TILES = 32
N_REP = 64


def draw_momentum(key, part):
    key = jax.random.fold_in(key, 11)
    keys = jax.random.split(key, 4)
    shape = (N_REP, TILES, TILE, TILE)
    base = jax.random.normal(keys[0], shape, jnp.float32)
    spread = math.log(10.0)
    tile_scale = jnp.exp(jax.random.uniform(keys[1], (1, TILES, 1, 1), jnp.float32, -0.5 * spread, 0.5 * spread))
    row_scale = jnp.exp(jax.random.uniform(keys[2], (1, TILES, TILE, 1), jnp.float32, -0.35, 0.35))
    col_scale = jnp.exp(jax.random.uniform(keys[3], (1, TILES, 1, TILE), jnp.float32, -0.35, 0.35))
    return jnp.clip(base * tile_scale * row_scale * col_scale, -12.0, 12.0)


def plant(entries, key, low, top_value):
    spot = [jax.random.randint(jax.random.fold_in(key, axis), (), 0, length) for axis, length in enumerate(entries.shape)]
    widest = entries.shape.index(max(entries.shape))
    neighbour = spot[:widest] + [(spot[widest] + 1) % entries.shape[widest]] + spot[widest + 1:]
    return entries.at[tuple(spot)].set(low).at[tuple(neighbour)].set(top_value)


def block_levels(own_key, shape, pieces, least, largest):
    def one(position, shards_of):
        heights = jax.random.uniform(jax.random.fold_in(jax.random.fold_in(own_key, 6), position), (shards_of,), jnp.float32, least / len(pieces), largest / len(pieces))
        return jnp.repeat(jnp.exp(heights), shape[position] // shards_of).reshape((-1,) + (1,) * (len(shape) - position - 1))

    gain = one(*pieces[0])
    for cut in pieces[1:]:
        gain = gain * one(*cut)
    return gain


def noise(own_key, extent, scale, most, shards=(), kind=jnp.bfloat16):
    gain = block_levels(own_key, extent, shards, -0.22, 0.18) if shards else 1.0
    result = jax.random.normal(own_key, extent, jnp.float32) * scale * gain
    return jnp.minimum(jnp.maximum(result, -most), most).astype(kind)


def setup_inputs(seed: int = 0) -> dict:
    key_list = jax.random.split(jax.random.key(seed), 5)
    return {
        "gradients": noise(key_list[0], (N_REP, TILES, TILE, TILE), 1.0, 6.0, ((0, 64), (1, 8))),
        "momentum": draw_momentum(jax.random.fold_in(key_list[4], 71), 0),
        "params": noise(key_list[2], (TILES, TILE, TILE), 0.5, 3.0, ((0, 8),)),
        "band_offsets": plant(jax.random.randint(key_list[3], (TILES, 2), 0, TILE - BAND + 1), jax.random.fold_in(key_list[3], 1), 0, TILE - BAND).astype(jnp.int32),
    }


def dct_entries(freq, length):
    kval = freq.astype(jnp.float32)[..., None]
    place = jnp.arange(length, dtype=jnp.float32)
    factor = jnp.where(kval == 0, math.sqrt(1.0 / length), math.sqrt(2.0 / length))
    return factor * jnp.cos(math.pi * (place + 0.5) * kval / length)

def band_tables(offsets, length, width):
    steps = jnp.arange(width, dtype=jnp.int32)
    rows_tab = dct_entries(offsets[:, 0:1].astype(jnp.int32) + steps[None, :], length)
    cols_tab = dct_entries(offsets[:, 1:2].astype(jnp.int32) + steps[None, :], length)
    return (rows_tab, cols_tab)

def reference(gradients, momentum, params, band_offsets):
    highest = lax.Precision.HIGHEST
    rows_tab, cols_tab = band_tables(band_offsets, TILE, BAND)
    moment = 0.9 * momentum + gradients.astype(jnp.float32)
    left = jnp.einsum('tik,rtkl->rtil', rows_tab, moment, precision=highest)
    bands = jnp.einsum('rtil,tjl->rtij', left, cols_tab, precision=highest)
    back = jnp.einsum('tik,rtij->rtkj', rows_tab, bands, precision=highest)
    local = jnp.einsum('rtkj,tjl->rtkl', back, cols_tab, precision=highest)
    new_momentum = moment - local
    average = lax.optimization_barrier(jnp.sum(bands, axis=0)) / N_REP
    half = jnp.einsum('tik,tij->tkj', rows_tab, average, precision=highest)
    update = jnp.einsum('tkj,tjl->tkl', half, cols_tab, precision=highest)
    scale = jnp.sqrt(lax.optimization_barrier(jnp.mean(update * update, axis=(1, 2), keepdims=True)) + 1e-06)
    new_params = (params.astype(jnp.float32) - update / scale).astype(jnp.bfloat16)
    return (new_momentum, new_params)
```

```python
import functools
import math

import jax
import jax.numpy as jnp
import numpy as np
from jax import lax
from jax.experimental import pallas as pl
from jax.experimental.pallas import tpu as pltpu
from jax.sharding import Mesh, PartitionSpec as P

BAND = 16
TILE = 128
AXES = ("yh", "z", "core", "x", "yl")
PLANE = ("yh", "core", "x", "yl")
F32 = jnp.float32
BF16 = jnp.bfloat16
ROWS = 96


def cosine_table():
    k = np.arange(TILE, dtype=np.float64)[:, None]
    x = np.arange(TILE, dtype=np.float64)[None, :]
    factor = np.where(k == 0, math.sqrt(1.0 / TILE), math.sqrt(2.0 / TILE))
    return factor * np.cos(math.pi * (x + 0.5) * k / TILE)


def split_table():
    table = cosine_table().astype(np.float32)
    high = table.astype(jnp.bfloat16)
    low = (table - high.astype(np.float32)).astype(jnp.bfloat16)
    across = np.concatenate([high, low], axis=1)
    down = np.concatenate([high.T, low.T], axis=0)
    return across, down


def iota(shape, dim):
    return lax.broadcasted_iota(jnp.int32, shape, dim)


def dot(a, b):
    return lax.dot_general(a, b, (((1,), (0,)), ((), ())), preferred_element_type=F32)


def dot_nt(a, b):
    return lax.dot_general(a, b, (((1,), (1,)), ((), ())), preferred_element_type=F32)


def pieces(v):
    high = v.astype(BF16)
    low = (v - high.astype(F32)).astype(BF16)
    return high, low


def fold(v):
    return v[:, :TILE] + v[:, TILE:]


def wide(v):
    high, low = pieces(v)
    return jnp.concatenate([high, low], axis=1)


def weights(v):
    both = wide(v)
    return jnp.concatenate([both, both], axis=0)


def frequencies(offs_ref, which):
    lane = iota((1, TILE), 1)
    tile = (lane % 64) // BAND
    freq = lane % BAND
    for t in range(4):
        freq = freq + jnp.where(tile == t, offs_ref[t, which], 0)
    return freq


def tables(freq, down):
    picks = (iota((TILE, TILE), 0) == freq).astype(F32).astype(BF16)
    both = dot(down, picks)
    return both[:TILE].astype(BF16), both[TILE:].astype(BF16)


def moments(g_ref, m_ref):
    return 0.9 * m_ref[...] + g_ref[...].astype(F32)


def bands_kernel(offs_ref, g_ref, m_ref, across_ref, down_ref, packed_ref, bands_ref):
    lane = iota((1, TILE), 1)
    slot = (lane % 64) // BAND
    cols_high, cols_low = tables(frequencies(offs_ref, 1), down_ref[...])
    cols = jnp.concatenate([cols_high, cols_low], axis=1)
    cols = jnp.concatenate([cols, cols], axis=0)
    steps = iota((BAND, TILE), 1) - iota((BAND, TILE), 0)
    picks = jnp.concatenate([(steps == offs_ref[t, 0]).astype(F32) for t in range(4)], axis=0)
    rows = dot(picks.astype(BF16), across_ref[...]).astype(BF16)
    right = jnp.zeros((TILE, TILE), F32)
    for t in range(4):
        moment = 0.9 * m_ref[t] + g_ref[t].astype(F32)
        right = jnp.where(slot == t, fold(dot(wide(moment), cols)), right)
    every = fold(dot(rows, weights(right)))
    bands = jnp.zeros((BAND, TILE), F32)
    for t in range(4):
        bands = jnp.where(slot == t, every[BAND * t : BAND * t + BAND], bands)
    bands_ref[...] = bands
    packed_ref[...] = jnp.where(lane < 64, bands[:8], bands[8:])


def momentum_kernel(offs_ref, g_ref, m_ref, down_ref, bands_ref, out_ref):
    lane = iota((1, TILE), 1)
    rows = jnp.concatenate(tables(frequencies(offs_ref, 0), down_ref[...]), axis=1)
    cols_high, cols_low = tables(frequencies(offs_ref, 1), down_ref[...])
    cols = jnp.concatenate(
        [jnp.concatenate([cols_high, cols_high], axis=1), jnp.concatenate([cols_low, cols_low], axis=1)], axis=0
    )
    bands = bands_ref[...]
    diagonal = [jnp.where(lane // BAND == t, bands, 0.0) for t in range(4)]
    diagonal = jnp.concatenate(diagonal + [jnp.zeros((64, TILE), F32)], axis=0)
    half = wide(fold(dot(rows, weights(diagonal))))
    lanes = iota((1, 2 * TILE), 1)
    slot = (lanes % TILE) // BAND
    for t in range(4):
        moment = 0.9 * m_ref[t] + g_ref[t].astype(F32)
        own = jnp.where(slot == t, half.astype(F32), 0.0).astype(BF16)
        out_ref[t] = moment - fold(dot_nt(own, cols))


def block_kernel(offs_ref, got_ref, params_ref, out_ref):
    lane = iota((1, TILE), 1)
    first = lane < 64
    total = jnp.sum(got_ref[...], axis=0)
    turned = pltpu.roll(total, 64, 1)
    high, low = [p.astype(F32) for p in pieces(total)]
    turned_high, turned_low = [p.astype(F32) for p in pieces(turned)]
    bands = jnp.concatenate(
        [jnp.where(first, high, turned_low), jnp.where(first, turned_high, low)], axis=0
    ).astype(BF16)
    row = iota((BAND, TILE), 0)
    freq = jnp.where(row == 0, frequencies(offs_ref, 0), frequencies(offs_ref, 1))
    tail = jnp.concatenate([bands, freq.astype(F32).astype(BF16)], axis=0)
    quarter = 2 * lax.axis_index("yh") + lax.axis_index("core")
    for core in range(2):
        piece = params_ref[4 * core + quarter]
        for yh in range(2):
            for s in range(8):
                out_ref[(2 * yh + core) * 8 + s, :64] = piece
                out_ref[(2 * yh + core) * 8 + s, 64:] = tail


def update_kernel(own_ref, other_ref, down_ref, out_ref):
    lane = iota((1, TILE), 1)
    first = lane < 64
    down = down_ref[...]
    core = lax.axis_index("core")
    lanes = iota((1, 2 * TILE), 1)
    slot = (lanes % TILE) // BAND
    groups = []
    squares = []
    for g in range(4):
        sums = []
        for s in (2 * g, 2 * g + 1):
            v = own_ref[s, 64:80].astype(F32)
            for q in range(1, 4):
                v = v + own_ref[8 * q + s, 64:80].astype(F32)
            v = (v + pltpu.roll(v, 64, 1)) * (1.0 / 64)
            sums.append(v)
        groups.append(sums)
        both = jnp.where(first, sums[0], sums[1])
        squares.append(jnp.sum(both * both, axis=0, keepdims=True))
    squares = jnp.concatenate(squares + squares, axis=0)
    same = (iota((TILE, TILE), 0) // BAND == iota((TILE, TILE), 1) // BAND).astype(F32).astype(BF16)
    high, low = pieces(squares)
    mean = (dot(high, same) + dot(low, same)) * (1.0 / (TILE * TILE))
    inverse = 1.0 / jnp.sqrt(mean + 1e-06)
    for g in range(4):
        freqs = [own_ref[s, 80:96].astype(F32).astype(jnp.int32) for s in (2 * g, 2 * g + 1)]
        freqs = jnp.where(first, freqs[0], freqs[1])
        rows = jnp.concatenate(tables(freqs[0:1], down), axis=1)
        cols_high, cols_low = tables(freqs[1:2], down)
        cols = jnp.concatenate(
            [jnp.concatenate([cols_high, cols_high], axis=1), jnp.concatenate([cols_low, cols_low], axis=1)], axis=0
        )
        scaled = [v * inverse[g : g + 1] for v in groups[g]]
        diagonal = jnp.concatenate([jnp.where(lane // BAND == t, scaled[t // 4], 0.0) for t in range(8)], axis=0)
        half = wide(fold(dot(rows, weights(diagonal)))).astype(F32)
        for ref, half_of in ((own_ref, core), (other_ref, 1 - core)):
            for sh in range(2):
                for yh in range(2):
                    s = 2 * g + sh
                    tile = 2 * half_of + yh
                    own = jnp.where(slot == 4 * sh + tile, half, 0.0).astype(BF16)
                    update = fold(dot_nt(own, cols))
                    params = jnp.concatenate([ref[16 * yh + s, :64], ref[16 * yh + 8 + s, :64]], axis=0)
                    out_ref[4 * s + tile] = (params.astype(F32) - update).astype(BF16)


SMEM = pl.BlockSpec(memory_space=pltpu.SMEM)
VMEM = pl.BlockSpec(memory_space=pltpu.VMEM)
PARAMS = pltpu.CompilerParams(vmem_limit_bytes=40 * 1024 * 1024)


def per_device(gradients, momentum, params, band_offsets):
    across, down = [jnp.asarray(t) for t in split_table()]
    g, m = gradients[0], momentum[0]
    packed, bands = pl.pallas_call(
        bands_kernel,
        out_shape=(jax.ShapeDtypeStruct((8, TILE), F32), jax.ShapeDtypeStruct((BAND, TILE), F32)),
        in_specs=[SMEM, VMEM, VMEM, VMEM, VMEM],
        out_specs=(VMEM, VMEM),
        compiler_params=PARAMS,
        name="bands",
    )(band_offsets, g, m, across, down)
    got = lax.all_to_all(jnp.broadcast_to(packed[None], (16, 8, TILE)), "z", 0, 0)
    blocks = pl.pallas_call(
        block_kernel,
        out_shape=jax.ShapeDtypeStruct((32, ROWS, TILE), BF16),
        in_specs=[SMEM, VMEM, VMEM],
        out_specs=VMEM,
        compiler_params=PARAMS,
        name="blocks",
    )(band_offsets, got, params.reshape(8, 64, TILE))
    own = lax.all_to_all(blocks, PLANE, 0, 0)
    other = lax.ppermute(own, "core", [(0, 1), (1, 0)])
    new_momentum = pl.pallas_call(
        momentum_kernel,
        out_shape=jax.ShapeDtypeStruct((4, TILE, TILE), F32),
        in_specs=[SMEM, VMEM, VMEM, VMEM, VMEM],
        out_specs=VMEM,
        compiler_params=PARAMS,
        cost_estimate=pl.CostEstimate(flops=200_000_000, bytes_accessed=700_000, transcendentals=0),
        name="momentum",
    )(band_offsets, g, m, down, bands)
    whole = pl.pallas_call(
        update_kernel,
        out_shape=jax.ShapeDtypeStruct((32, TILE, TILE), BF16),
        in_specs=[VMEM, VMEM, VMEM],
        out_specs=VMEM,
        compiler_params=PARAMS,
        name="update",
    )(own, other, down)
    return (new_momentum[None], whole)


def solution(mesh):
    fine = Mesh(mesh.devices.reshape(2, 16, 2, 4, 2), AXES)
    rep, shard = ("yh", "z", "core"), ("x", "yl")
    in_specs = (P(rep, shard, None, None), P(rep, shard, None, None), P(shard, None, None), P(shard, None))
    out_specs = (P(rep, shard, None, None), P())
    return jax.shard_map(per_device, mesh=fine, in_specs=in_specs, out_specs=out_specs, check_vma=False)
```

```python
import functools
import math

import jax
import jax.numpy as jnp
import numpy as np
from jax import lax
from jax.experimental import pallas as pl
from jax.experimental.pallas import tpu as pltpu
from jax.sharding import Mesh, PartitionSpec as P

BAND = 16
TILE = 128
AXES = ("yh", "z", "core", "x", "yl")
PLANE = ("yh", "x", "yl")
F32 = jnp.float32
BF16 = jnp.bfloat16
ROWS = 160


def cosine_table():
    k = np.arange(TILE, dtype=np.float64)[:, None]
    x = np.arange(TILE, dtype=np.float64)[None, :]
    factor = np.where(k == 0, math.sqrt(1.0 / TILE), math.sqrt(2.0 / TILE))
    return factor * np.cos(math.pi * (x + 0.5) * k / TILE)


def split_table():
    table = cosine_table().astype(np.float32)
    high = table.astype(jnp.bfloat16)
    low = (table - high.astype(np.float32)).astype(jnp.bfloat16)
    return np.concatenate([high.T, low.T], axis=0)


def iota(shape, dim):
    return lax.broadcasted_iota(jnp.int32, shape, dim)


def dot(a, b):
    return lax.dot_general(a, b, (((1,), (0,)), ((), ())), preferred_element_type=F32)


def dot_nt(a, b):
    return lax.dot_general(a, b, (((1,), (1,)), ((), ())), preferred_element_type=F32)


def pieces(v):
    high = v.astype(BF16)
    low = (v - high.astype(F32)).astype(BF16)
    return high, low


def fold(v):
    return v[:, :TILE] + v[:, TILE:]


def wide(v):
    high, low = pieces(v)
    return jnp.concatenate([high, low], axis=1)


def weights(v):
    both = wide(v)
    return jnp.concatenate([both, both], axis=0)


def frequencies(offs_ref, which):
    lane = iota((1, TILE), 1)
    tile = (lane % 64) // BAND
    freq = lane % BAND
    for t in range(4):
        freq = freq + jnp.where(tile == t, offs_ref[which, t], 0)
    return freq


def tables(freq, down):
    picks = (iota((TILE, TILE), 0) == freq).astype(F32).astype(BF16)
    both = dot(down, picks)
    return both[:TILE].astype(BF16), both[TILE:].astype(BF16)


def masks(count, dtype):
    lanes = iota((1, 2 * TILE), 1)
    return [((lanes % TILE) // BAND == t).astype(F32).astype(dtype) for t in range(count)]


def stacked(high, low):
    return jnp.concatenate(
        [jnp.concatenate([high, high], axis=1), jnp.concatenate([low, low], axis=1)], axis=0
    )


def bands_kernel(
    offs_hbm, g_hbm, m_hbm, down_hbm, packed_ref, bands_ref, freq_ref, rows_ref, cols_ref, offs_ref, g_ref, m_ref, down_ref, sems
):
    copies = [
        pltpu.make_async_copy(src, dst, sems.at[i])
        for i, (src, dst) in enumerate(
            ((offs_hbm, offs_ref), (down_hbm, down_ref), (m_hbm, m_ref), (g_hbm, g_ref))
        )
    ]
    for copy in copies:
        copy.start()
    lane = iota((1, TILE), 1)
    slot = (lane % 64) // BAND
    copies[0].wait()
    row_freq, col_freq = frequencies(offs_ref, 0), frequencies(offs_ref, 1)
    steps = iota((BAND, TILE), 1) - iota((BAND, TILE), 0)
    picks = jnp.concatenate([(steps == offs_ref[0, t]).astype(F32) for t in range(4)], axis=0)
    copies[1].wait()
    down = down_ref[...]
    cols_high, cols_low = tables(col_freq, down)
    cols = jnp.concatenate([cols_high, cols_low], axis=1)
    cols_ref[...] = stacked(cols_high, cols_low)
    cols = jnp.concatenate([cols, cols], axis=0)
    rows = dot_nt(picks.astype(BF16), down).astype(BF16)
    rows_ref[...] = jnp.concatenate(tables(row_freq, down), axis=1)
    row = iota((BAND, TILE), 0)
    freq_ref[...] = jnp.where(row == 0, row_freq, col_freq).astype(F32).astype(BF16)
    copies[2].wait()
    copies[3].wait()
    right = jnp.zeros((TILE, TILE), F32)
    for t in range(4):
        moment = 0.9 * m_ref[t] + g_ref[t].astype(F32)
        right = jnp.where(slot == t, fold(dot(wide(moment), cols)), right)
    every = fold(dot(rows, weights(right)))
    bands = jnp.zeros((BAND, TILE), F32)
    for t in range(4):
        bands = jnp.where(slot == t, every[BAND * t : BAND * t + BAND], bands)
    bands_ref[...] = bands
    packed_ref[...] = jnp.where(lane < 64, bands[:8], bands[8:])


def block_kernel(got_ref, params_ref, freq_ref, out_ref):
    first = iota((1, TILE), 1) < 64
    total = jnp.sum(got_ref[...], axis=0)
    turned = pltpu.roll(total, 64, 1)
    high, low = [p.astype(F32) for p in pieces(total)]
    turned_high, turned_low = [p.astype(F32) for p in pieces(turned)]
    bands = jnp.concatenate(
        [jnp.where(first, high, turned_low), jnp.where(first, turned_high, low)], axis=0
    ).astype(BF16)
    block = params_ref[2 * lax.axis_index("core") + lax.axis_index("yh")]
    freq = freq_ref[...]
    for d in range(16):
        out_ref[d, :128] = block
        out_ref[d, 128:144] = bands
        out_ref[d, 144:] = freq


def momentum_kernel(g_ref, m_ref, bands_ref, rows_ref, cols_ref, got_ref, down_ref, out_ref, all_rows_ref, all_cols_ref):
    lane = iota((1, TILE), 1)
    bands = bands_ref[...]
    diagonal = [jnp.where(lane // BAND == t, bands, 0.0) for t in range(4)]
    diagonal = jnp.concatenate(diagonal + [jnp.zeros((64, TILE), F32)], axis=0)
    half = wide(fold(dot(rows_ref[...], weights(diagonal))))
    cols = cols_ref[...]
    for t, mask in enumerate(masks(4, BF16)):
        moment = 0.9 * m_ref[t] + g_ref[t].astype(F32)
        out_ref[t] = moment - fold(dot_nt(half * mask, cols))
    down = down_ref[...]
    for g in range(4):
        freqs = [got_ref[s, 144:160].astype(F32).astype(jnp.int32) for s in (2 * g, 2 * g + 1)]
        freqs = jnp.where(lane < 64, freqs[0], freqs[1])
        all_rows_ref[g] = jnp.concatenate(tables(freqs[0:1], down), axis=1)
        all_cols_ref[g] = stacked(*tables(freqs[1:2], down))


def update_kernel(own_ref, other_ref, rows_ref, cols_ref, out_hbm, out_ref, sems):
    lane = iota((1, TILE), 1)
    first = lane < 64
    core = lax.axis_index("core")
    groups = []
    squares = []
    for g in range(4):
        sums = []
        for s in (2 * g, 2 * g + 1):
            v = sum(ref[i, 128:144].astype(F32) for ref in (own_ref, other_ref) for i in (s, 8 + s))
            sums.append((v + pltpu.roll(v, 64, 1)) * (1.0 / 64))
        groups.append(sums)
        both = jnp.where(first, sums[0], sums[1])
        squares.append(jnp.sum(both * both, axis=0, keepdims=True))
    squares = jnp.concatenate(squares + squares, axis=0)
    same = (iota((TILE, TILE), 0) // BAND == iota((TILE, TILE), 1) // BAND).astype(F32).astype(BF16)
    high, low = pieces(squares)
    mean = (dot(high, same) + dot(low, same)) * (1.0 / (TILE * TILE))
    inverse = 1.0 / jnp.sqrt(mean + 1e-06)
    lanes = (iota((1, 2 * TILE), 1) % TILE) // BAND
    copies = []
    for g in range(4):
        scaled = [v * inverse[g : g + 1] for v in groups[g]]
        diagonal = jnp.concatenate([jnp.where(lane // BAND == t, scaled[t // 4], 0.0) for t in range(8)], axis=0)
        half = wide(fold(dot(rows_ref[g], weights(diagonal))))
        cols = cols_ref[g]
        for ref, half_of in ((own_ref, core), (other_ref, 1 - core)):
            for sh in range(2):
                for yh in range(2):
                    s = 2 * g + sh
                    tile = 2 * half_of + yh
                    mask = (lanes == 4 * sh + tile).astype(F32).astype(BF16)
                    update = fold(dot_nt(half * mask, cols))
                    params = ref[8 * yh + s, :128].astype(F32)
                    out_ref[4 * s + tile] = (params - update).astype(BF16)
        copies.append(
            pltpu.make_async_copy(out_ref.at[pl.ds(8 * g, 8)], out_hbm.at[pl.ds(8 * g, 8)], sems.at[g])
        )
        copies[-1].start()
    for copy in copies:
        copy.wait()


SMEM = pl.BlockSpec(memory_space=pltpu.SMEM)
VMEM = pl.BlockSpec(memory_space=pltpu.VMEM)
HBM = pl.BlockSpec(memory_space=pltpu.HBM)
PARAMS = pltpu.CompilerParams(vmem_limit_bytes=40 * 1024 * 1024)
shape = jax.ShapeDtypeStruct


def per_device(gradients, momentum, params, band_offsets):
    down = jnp.asarray(split_table())
    g, m = gradients[0], momentum[0]
    packed, bands, freq, rows, cols = pl.pallas_call(
        bands_kernel,
        out_shape=(
            shape((8, TILE), F32),
            shape((BAND, TILE), F32),
            shape((BAND, TILE), BF16),
            shape((TILE, 2 * TILE), BF16),
            shape((2 * TILE, 2 * TILE), BF16),
        ),
        in_specs=[HBM] * 4,
        out_specs=(VMEM,) * 5,
        scratch_shapes=[
            pltpu.SMEM((2, 4), jnp.int32),
            pltpu.VMEM((4, TILE, TILE), BF16),
            pltpu.VMEM((4, TILE, TILE), F32),
            pltpu.VMEM((2 * TILE, TILE), BF16),
            pltpu.SemaphoreType.DMA((4,)),
        ],
        compiler_params=pltpu.CompilerParams(vmem_limit_bytes=16 * 1024 * 1024),
        name="bands",
    )(*[pltpu.with_memory_space_constraint(a, pltpu.HBM) for a in (band_offsets.T, g, m, down)])
    got = lax.all_to_all(jnp.broadcast_to(packed[None], (16, 8, TILE)), "z", 0, 0)
    blocks = pl.pallas_call(
        block_kernel,
        out_shape=shape((16, ROWS, TILE), BF16),
        in_specs=[VMEM] * 3,
        out_specs=VMEM,
        compiler_params=PARAMS,
        name="blocks",
    )(got, params, freq)
    own = lax.all_to_all(blocks, PLANE, 0, 0)
    other = lax.ppermute(own, "core", [(0, 1), (1, 0)])
    new_momentum, all_rows, all_cols = pl.pallas_call(
        momentum_kernel,
        out_shape=(
            shape((4, TILE, TILE), F32),
            shape((4, TILE, 2 * TILE), BF16),
            shape((4, 2 * TILE, 2 * TILE), BF16),
        ),
        in_specs=[VMEM] * 7,
        out_specs=(VMEM,) * 3,
        compiler_params=PARAMS,
        cost_estimate=pl.CostEstimate(flops=200_000_000, bytes_accessed=700_000, transcendentals=0),
        name="momentum",
    )(g, m, bands, rows, cols, own, down)
    whole = pl.pallas_call(
        update_kernel,
        out_shape=shape((32, TILE, TILE), BF16),
        in_specs=[VMEM] * 4,
        out_specs=HBM,
        scratch_shapes=[pltpu.VMEM((32, TILE, TILE), BF16), pltpu.SemaphoreType.DMA((4,))],
        compiler_params=PARAMS,
        name="update",
    )(own, other, all_rows, all_cols)
    return (new_momentum[None], whole)


def solution(mesh):
    fine = Mesh(mesh.devices.reshape(2, 16, 2, 4, 2), AXES)
    rep, shard = ("yh", "z", "core"), ("x", "yl")
    in_specs = (P(rep, shard, None, None), P(rep, shard, None, None), P(shard, None, None), P(shard, None))
    out_specs = (P(rep, shard, None, None), P())
    return jax.shard_map(per_device, mesh=fine, in_specs=in_specs, out_specs=out_specs, check_vma=False)
```

```python
import functools
import math

import jax
import jax.numpy as jnp
import numpy as np
from jax import lax
from jax.experimental import pallas as pl
from jax.experimental.pallas import tpu as pltpu
from jax.sharding import Mesh, PartitionSpec as P

BAND = 16
TILE = 128
AXES = ("yh", "z", "core", "x", "yl")
PLANE = ("yh", "yl", "x")
F32 = jnp.float32
BF16 = jnp.bfloat16
ROWS = 160


def cosine_table():
    k = np.arange(TILE, dtype=np.float64)[:, None]
    x = np.arange(TILE, dtype=np.float64)[None, :]
    factor = np.where(k == 0, math.sqrt(1.0 / TILE), math.sqrt(2.0 / TILE))
    return factor * np.cos(math.pi * (x + 0.5) * k / TILE)


def split_table():
    table = cosine_table().astype(np.float32)
    high = table.astype(jnp.bfloat16)
    low = (table - high.astype(np.float32)).astype(jnp.bfloat16)
    return np.concatenate([high.T, low.T], axis=0)


def iota(shape, dim):
    return lax.broadcasted_iota(jnp.int32, shape, dim)


def dot(a, b):
    return lax.dot_general(a, b, (((1,), (0,)), ((), ())), preferred_element_type=F32)


def dot_nt(a, b):
    return lax.dot_general(a, b, (((1,), (1,)), ((), ())), preferred_element_type=F32)


def pieces(v):
    high = v.astype(BF16)
    low = (v - high.astype(F32)).astype(BF16)
    return high, low


def fold(v):
    return v[:, :TILE] + v[:, TILE:]


def wide(v):
    high, low = pieces(v)
    return jnp.concatenate([high, low], axis=1)


def weights(v):
    both = wide(v)
    return jnp.concatenate([both, both], axis=0)


def frequencies(offs_ref, which):
    lane = iota((1, TILE), 1)
    tile = (lane % 64) // BAND
    freq = lane % BAND
    for t in range(4):
        freq = freq + jnp.where(tile == t, offs_ref[which, t], 0)
    return freq


def tables(freq, down):
    picks = (iota((TILE, TILE), 0) == freq).astype(F32).astype(BF16)
    both = dot(down, picks)
    return both[:TILE].astype(BF16), both[TILE:].astype(BF16)


def masks(count, dtype):
    lanes = iota((1, 2 * TILE), 1)
    return [((lanes % TILE) // BAND == t).astype(F32).astype(dtype) for t in range(count)]


def stacked(high, low):
    return jnp.concatenate(
        [jnp.concatenate([high, high], axis=1), jnp.concatenate([low, low], axis=1)], axis=0
    )


def bands_kernel(
    offs_hbm, g_hbm, m_hbm, down_hbm, packed_ref, bands_ref, freq_ref, rows_ref, cols_ref, offs_ref, g_ref, m_ref, down_ref, sems
):
    copies = [
        pltpu.make_async_copy(src, dst, sems.at[i])
        for i, (src, dst) in enumerate(
            ((offs_hbm, offs_ref), (down_hbm, down_ref), (m_hbm, m_ref), (g_hbm, g_ref))
        )
    ]
    for copy in copies:
        copy.start()
    lane = iota((1, TILE), 1)
    slot = (lane % 64) // BAND
    copies[0].wait()
    row_freq, col_freq = frequencies(offs_ref, 0), frequencies(offs_ref, 1)
    steps = iota((BAND, TILE), 1) - iota((BAND, TILE), 0)
    picks = jnp.concatenate([(steps == offs_ref[0, t]).astype(F32) for t in range(4)], axis=0)
    copies[1].wait()
    down = down_ref[...]
    cols_high, cols_low = tables(col_freq, down)
    cols = jnp.concatenate([cols_high, cols_low], axis=1)
    cols_ref[...] = stacked(cols_high, cols_low)
    cols = jnp.concatenate([cols, cols], axis=0)
    rows = dot_nt(picks.astype(BF16), down).astype(BF16)
    rows_ref[...] = jnp.concatenate(tables(row_freq, down), axis=1)
    row = iota((BAND, TILE), 0)
    freq_ref[...] = jnp.where(row == 0, row_freq, col_freq).astype(F32).astype(BF16)
    copies[2].wait()
    copies[3].wait()
    right = jnp.zeros((TILE, TILE), F32)
    for t in range(4):
        moment = 0.9 * m_ref[t] + g_ref[t].astype(F32)
        right = jnp.where(slot == t, fold(dot(wide(moment), cols)), right)
    every = fold(dot(rows, weights(right)))
    bands = jnp.zeros((BAND, TILE), F32)
    for t in range(4):
        bands = jnp.where(slot == t, every[BAND * t : BAND * t + BAND], bands)
    bands_ref[...] = bands
    packed_ref[...] = jnp.where(lane < 64, bands[:8], bands[8:])


def block_kernel(got_ref, params_ref, freq_ref, out_ref):
    first = iota((1, TILE), 1) < 64
    total = jnp.sum(got_ref[...], axis=0)
    turned = pltpu.roll(total, 64, 1)
    high, low = [p.astype(F32) for p in pieces(total)]
    turned_high, turned_low = [p.astype(F32) for p in pieces(turned)]
    bands = jnp.concatenate(
        [jnp.where(first, high, turned_low), jnp.where(first, turned_high, low)], axis=0
    ).astype(BF16)
    block = params_ref[2 * lax.axis_index("core") + lax.axis_index("yh")]
    freq = freq_ref[...]
    for d in range(16):
        out_ref[d, :128] = block
        out_ref[d, 128:144] = bands
        out_ref[d, 144:] = freq


def source(yh, s):
    return 8 * yh + 4 * (s % 2) + s // 2


def momentum_kernel(g_ref, m_ref, bands_ref, rows_ref, cols_ref, got_ref, down_ref, out_ref, all_rows_ref, all_cols_ref):
    lane = iota((1, TILE), 1)
    bands = bands_ref[...]
    diagonal = [jnp.where(lane // BAND == t, bands, 0.0) for t in range(4)]
    diagonal = jnp.concatenate(diagonal + [jnp.zeros((64, TILE), F32)], axis=0)
    half = wide(fold(dot(rows_ref[...], weights(diagonal))))
    cols = cols_ref[...]
    for t, mask in enumerate(masks(4, BF16)):
        moment = 0.9 * m_ref[t] + g_ref[t].astype(F32)
        out_ref[t] = moment - fold(dot_nt(half * mask, cols))
    down = down_ref[...]
    for g in range(4):
        freqs = [got_ref[source(0, s), 144:160].astype(F32).astype(jnp.int32) for s in (2 * g, 2 * g + 1)]
        freqs = jnp.where(lane < 64, freqs[0], freqs[1])
        all_rows_ref[g] = jnp.concatenate(tables(freqs[0:1], down), axis=1)
        picks = (iota((TILE, TILE), 0) == freqs[1:2]).astype(F32).T.astype(BF16)
        all_cols_ref[g] = dot_nt(picks, down).astype(BF16)


def update_kernel(own_ref, other_ref, rows_ref, cols_ref, out_hbm, out_ref, sems):
    lane = iota((1, TILE), 1)
    first = lane < 64
    core = lax.axis_index("core")
    halves = []
    squares = []
    for g in range(4):
        sums = []
        for s in (2 * g, 2 * g + 1):
            v = sum(ref[source(yh, s), 128:144].astype(F32) for ref in (own_ref, other_ref) for yh in range(2))
            sums.append((v + pltpu.roll(v, 64, 1)) * (1.0 / 64))
        both = jnp.where(first, sums[0], sums[1])
        squares.append(jnp.sum(both * both, axis=0, keepdims=True))
        diagonal = jnp.concatenate([jnp.where(lane // BAND == t, sums[t // 4], 0.0) for t in range(8)], axis=0)
        halves.append(fold(dot(rows_ref[g], weights(diagonal))))
    squares = jnp.concatenate(squares + squares, axis=0)
    same = (iota((TILE, TILE), 0) // BAND == iota((TILE, TILE), 1) // BAND).astype(F32).astype(BF16)
    high, low = pieces(squares)
    mean = (dot(high, same) + dot(low, same)) * (1.0 / (TILE * TILE))
    inverse = 1.0 / jnp.sqrt(mean + 1e-06)
    lanes = (iota((1, 2 * TILE), 1) % TILE) // BAND
    order = [(ref, half_of, sh, yh) for ref, half_of in ((own_ref, core), (other_ref, 1 - core)) for sh in range(2) for yh in range(2)]
    copies = []
    for g in range(4):
        half = wide(halves[g] * inverse[g : g + 1])
        left = jnp.concatenate(
            [half * (lanes == 4 * sh + 2 * half_of + yh).astype(F32).astype(BF16) for _, half_of, sh, yh in order], axis=0
        )
        cols = cols_ref[g]
        update = fold(dot(left, jnp.concatenate([cols, cols], axis=0)))
        for i, (ref, half_of, sh, yh) in enumerate(order):
            s = 2 * g + sh
            params = ref[source(yh, s), :128].astype(F32)
            out_ref[4 * s + 2 * half_of + yh] = (params - update[TILE * i : TILE * i + TILE]).astype(BF16)
        copies.append(
            pltpu.make_async_copy(out_ref.at[pl.ds(8 * g, 8)], out_hbm.at[pl.ds(8 * g, 8)], sems.at[g])
        )
        copies[-1].start()
    for copy in copies:
        copy.wait()


SMEM = pl.BlockSpec(memory_space=pltpu.SMEM)
VMEM = pl.BlockSpec(memory_space=pltpu.VMEM)
HBM = pl.BlockSpec(memory_space=pltpu.HBM)
PARAMS = pltpu.CompilerParams(vmem_limit_bytes=40 * 1024 * 1024)
shape = jax.ShapeDtypeStruct


def per_device(gradients, momentum, params, band_offsets):
    down = jnp.asarray(split_table())
    g, m = gradients[0], momentum[0]
    packed, bands, freq, rows, cols = pl.pallas_call(
        bands_kernel,
        out_shape=(
            shape((8, TILE), F32),
            shape((BAND, TILE), F32),
            shape((BAND, TILE), BF16),
            shape((TILE, 2 * TILE), BF16),
            shape((2 * TILE, 2 * TILE), BF16),
        ),
        in_specs=[HBM] * 4,
        out_specs=(VMEM,) * 5,
        scratch_shapes=[
            pltpu.SMEM((2, 4), jnp.int32),
            pltpu.VMEM((4, TILE, TILE), BF16),
            pltpu.VMEM((4, TILE, TILE), F32),
            pltpu.VMEM((2 * TILE, TILE), BF16),
            pltpu.SemaphoreType.DMA((4,)),
        ],
        compiler_params=pltpu.CompilerParams(vmem_limit_bytes=16 * 1024 * 1024),
        name="bands",
    )(*[pltpu.with_memory_space_constraint(a, pltpu.HBM) for a in (band_offsets.T, g, m, down)])
    got = lax.all_to_all(jnp.broadcast_to(packed[None], (16, 8, TILE)), "z", 0, 0)
    blocks = pl.pallas_call(
        block_kernel,
        out_shape=shape((16, ROWS, TILE), BF16),
        in_specs=[VMEM] * 3,
        out_specs=VMEM,
        compiler_params=PARAMS,
        name="blocks",
    )(got, params, freq)
    own = lax.all_to_all(blocks, PLANE, 0, 0)
    other = lax.ppermute(own, "core", [(0, 1), (1, 0)])
    new_momentum, all_rows, all_cols = pl.pallas_call(
        momentum_kernel,
        out_shape=(
            shape((4, TILE, TILE), F32),
            shape((4, TILE, 2 * TILE), BF16),
            shape((4, TILE, 2 * TILE), BF16),
        ),
        in_specs=[VMEM] * 7,
        out_specs=(VMEM,) * 3,
        compiler_params=PARAMS,
        cost_estimate=pl.CostEstimate(flops=200_000_000, bytes_accessed=700_000, transcendentals=0),
        name="momentum",
    )(g, m, bands, rows, cols, own, down)
    whole = pl.pallas_call(
        update_kernel,
        out_shape=shape((32, TILE, TILE), BF16),
        in_specs=[VMEM] * 4,
        out_specs=HBM,
        scratch_shapes=[pltpu.VMEM((32, TILE, TILE), BF16), pltpu.SemaphoreType.DMA((4,))],
        compiler_params=PARAMS,
        name="update",
    )(own, other, all_rows, all_cols)
    return (new_momentum[None], whole)


def solution(mesh):
    fine = Mesh(mesh.devices.reshape(2, 16, 2, 4, 2), AXES)
    rep, shard = ("yh", "z", "core"), ("x", "yl")
    in_specs = (P(rep, shard, None, None), P(rep, shard, None, None), P(shard, None, None), P(shard, None))
    out_specs = (P(rep, shard, None, None), P())
    return jax.shard_map(per_device, mesh=fine, in_specs=in_specs, out_specs=out_specs, check_vma=False)
```

```python
import functools
import math

import jax
import jax.numpy as jnp
import numpy as np
from jax import lax
from jax.experimental import pallas as pl
from jax.experimental.pallas import tpu as pltpu
from jax.sharding import Mesh, PartitionSpec as P

BAND = 16
TILE = 128
AXES = ("yh", "z", "core", "x", "yl")
PLANE = ("yh", "yl", "x")
F32 = jnp.float32
BF16 = jnp.bfloat16
ROWS = 160


def cosine_table():
    k = np.arange(TILE, dtype=np.float64)[:, None]
    x = np.arange(TILE, dtype=np.float64)[None, :]
    factor = np.where(k == 0, math.sqrt(1.0 / TILE), math.sqrt(2.0 / TILE))
    return factor * np.cos(math.pi * (x + 0.5) * k / TILE)


def split_table():
    table = cosine_table().astype(np.float32)
    high = table.astype(jnp.bfloat16)
    low = (table - high.astype(np.float32)).astype(jnp.bfloat16)
    return np.concatenate([high.T, low.T], axis=0)


def iota(shape, dim):
    return lax.broadcasted_iota(jnp.int32, shape, dim)


def dot(a, b):
    return lax.dot_general(a, b, (((1,), (0,)), ((), ())), preferred_element_type=F32)


def dot_nt(a, b):
    return lax.dot_general(a, b, (((1,), (1,)), ((), ())), preferred_element_type=F32)


def pieces(v):
    high = v.astype(BF16)
    low = (v - high.astype(F32)).astype(BF16)
    return high, low


def fold(v):
    return v[:, :TILE] + v[:, TILE:]


def wide(v):
    high, low = pieces(v)
    return jnp.concatenate([high, low], axis=1)


def weights(v):
    both = wide(v)
    return jnp.concatenate([both, both], axis=0)


def frequencies(offs_ref, which):
    lane = iota((1, TILE), 1)
    tile = (lane % 64) // BAND
    freq = lane % BAND
    for t in range(4):
        freq = freq + jnp.where(tile == t, offs_ref[which, t], 0)
    return freq


def tables(freq, down):
    picks = (iota((TILE, TILE), 0) == freq).astype(F32).astype(BF16)
    both = dot(down, picks)
    return both[:TILE].astype(BF16), both[TILE:].astype(BF16)


def masks(count, dtype):
    lanes = iota((1, 2 * TILE), 1)
    return [((lanes % TILE) // BAND == t).astype(F32).astype(dtype) for t in range(count)]


def stacked(high, low):
    return jnp.concatenate(
        [jnp.concatenate([high, high], axis=1), jnp.concatenate([low, low], axis=1)], axis=0
    )


def bands_kernel(
    offs_hbm, g_hbm, m_hbm, down_hbm, packed_ref, bands_ref, freq_ref, rows_ref, cols_ref, offs_ref, g_ref, m_ref, down_ref, sems
):
    copies = [
        pltpu.make_async_copy(src, dst, sems.at[i])
        for i, (src, dst) in enumerate(
            ((offs_hbm, offs_ref), (down_hbm, down_ref), (m_hbm, m_ref), (g_hbm, g_ref))
        )
    ]
    for copy in copies:
        copy.start()
    lane = iota((1, TILE), 1)
    slot = (lane % 64) // BAND
    copies[0].wait()
    row_freq, col_freq = frequencies(offs_ref, 0), frequencies(offs_ref, 1)
    steps = iota((BAND, TILE), 1) - iota((BAND, TILE), 0)
    picks = jnp.concatenate([(steps == offs_ref[0, t]).astype(F32) for t in range(4)], axis=0)
    copies[1].wait()
    down = down_ref[...]
    cols_high, cols_low = tables(col_freq, down)
    cols = jnp.concatenate([cols_high, cols_low], axis=1)
    cols_ref[...] = stacked(cols_high, cols_low)
    cols = jnp.concatenate([cols, cols], axis=0)
    rows = dot_nt(picks.astype(BF16), down).astype(BF16)
    rows_ref[...] = jnp.concatenate(tables(row_freq, down), axis=1)
    row = iota((BAND, TILE), 0)
    freq_ref[...] = jnp.where(row == 0, row_freq, col_freq).astype(F32).astype(BF16)
    copies[2].wait()
    copies[3].wait()
    right = jnp.zeros((TILE, TILE), F32)
    for t in range(4):
        moment = 0.9 * m_ref[t] + g_ref[t].astype(F32)
        right = jnp.where(slot == t, fold(dot(wide(moment), cols)), right)
    every = fold(dot(rows, weights(right)))
    bands = jnp.zeros((BAND, TILE), F32)
    for t in range(4):
        bands = jnp.where(slot == t, every[BAND * t : BAND * t + BAND], bands)
    bands_ref[...] = bands
    packed_ref[...] = jnp.where(lane < 64, bands[:8], bands[8:])


def block_kernel(got_ref, params_ref, freq_ref, out_ref):
    first = iota((1, TILE), 1) < 64
    total = jnp.sum(got_ref[...], axis=0)
    turned = pltpu.roll(total, 64, 1)
    high, low = [p.astype(F32) for p in pieces(total)]
    turned_high, turned_low = [p.astype(F32) for p in pieces(turned)]
    bands = jnp.concatenate(
        [jnp.where(first, high, turned_low), jnp.where(first, turned_high, low)], axis=0
    ).astype(BF16)
    block = params_ref[2 * lax.axis_index("core") + lax.axis_index("yh")]
    freq = freq_ref[...]
    for d in range(16):
        out_ref[d, :128] = block
        out_ref[d, 128:144] = bands
        out_ref[d, 144:] = freq


def source(yh, s):
    return 15 - (8 * yh + 4 * (s % 2) + s // 2)


def momentum_kernel(g_ref, m_ref, bands_ref, rows_ref, cols_ref, got_ref, down_ref, out_ref, all_rows_ref, all_cols_ref):
    lane = iota((1, TILE), 1)
    bands = bands_ref[...]
    diagonal = [jnp.where(lane // BAND == t, bands, 0.0) for t in range(4)]
    diagonal = jnp.concatenate(diagonal + [jnp.zeros((64, TILE), F32)], axis=0)
    half = wide(fold(dot(rows_ref[...], weights(diagonal))))
    cols = cols_ref[...]
    for t, mask in enumerate(masks(4, BF16)):
        moment = 0.9 * m_ref[t] + g_ref[t].astype(F32)
        out_ref[t] = moment - fold(dot_nt(half * mask, cols))
    down = down_ref[...]
    for g in range(4):
        freqs = [got_ref[source(0, s), 144:160].astype(F32).astype(jnp.int32) for s in (2 * g, 2 * g + 1)]
        freqs = jnp.where(lane < 64, freqs[0], freqs[1])
        all_rows_ref[g] = jnp.concatenate(tables(freqs[0:1], down), axis=1)
        picks = (iota((TILE, TILE), 0) == freqs[1:2]).astype(F32).T.astype(BF16)
        all_cols_ref[g] = dot_nt(picks, down).astype(BF16)


def update_kernel(own_ref, other_ref, rows_ref, cols_ref, out_hbm, out_ref, sems):
    lane = iota((1, TILE), 1)
    first = lane < 64
    core = lax.axis_index("core")
    halves = []
    squares = []
    for g in range(4):
        sums = []
        for s in (2 * g, 2 * g + 1):
            v = sum(ref[source(yh, s), 128:144].astype(F32) for ref in (own_ref, other_ref) for yh in range(2))
            sums.append((v + pltpu.roll(v, 64, 1)) * (1.0 / 64))
        both = jnp.where(first, sums[0], sums[1])
        squares.append(jnp.sum(both * both, axis=0, keepdims=True))
        diagonal = jnp.concatenate([jnp.where(lane // BAND == t, sums[t // 4], 0.0) for t in range(8)], axis=0)
        halves.append(fold(dot(rows_ref[g], weights(diagonal))))
    squares = jnp.concatenate(squares + squares, axis=0)
    same = (iota((TILE, TILE), 0) // BAND == iota((TILE, TILE), 1) // BAND).astype(F32).astype(BF16)
    high, low = pieces(squares)
    mean = (dot(high, same) + dot(low, same)) * (1.0 / (TILE * TILE))
    inverse = 1.0 / jnp.sqrt(mean + 1e-06)
    lanes = (iota((1, 2 * TILE), 1) % TILE) // BAND
    order = [(ref, half_of, sh, yh) for ref, half_of in ((own_ref, core), (other_ref, 1 - core)) for sh in range(2) for yh in range(2)]
    copies = []
    for g in range(4):
        half = wide(halves[g] * inverse[g : g + 1])
        left = jnp.concatenate(
            [half * (lanes == 4 * sh + 2 * half_of + yh).astype(F32).astype(BF16) for _, half_of, sh, yh in order], axis=0
        )
        cols = cols_ref[g]
        update = fold(dot(left, jnp.concatenate([cols, cols], axis=0)))
        for i, (ref, half_of, sh, yh) in enumerate(order):
            s = 2 * g + sh
            params = ref[source(yh, s), :128].astype(F32)
            out_ref[4 * s + 2 * half_of + yh] = (params - update[TILE * i : TILE * i + TILE]).astype(BF16)
        copies.append(
            pltpu.make_async_copy(out_ref.at[pl.ds(8 * g, 8)], out_hbm.at[pl.ds(8 * g, 8)], sems.at[g])
        )
        copies[-1].start()
    for copy in copies:
        copy.wait()


SMEM = pl.BlockSpec(memory_space=pltpu.SMEM)
VMEM = pl.BlockSpec(memory_space=pltpu.VMEM)
HBM = pl.BlockSpec(memory_space=pltpu.HBM)
PARAMS = pltpu.CompilerParams(vmem_limit_bytes=40 * 1024 * 1024)
shape = jax.ShapeDtypeStruct


def per_device(gradients, momentum, params, band_offsets):
    down = jnp.asarray(split_table())
    g, m = gradients[0], momentum[0]
    packed, bands, freq, rows, cols = pl.pallas_call(
        bands_kernel,
        out_shape=(
            shape((8, TILE), F32),
            shape((BAND, TILE), F32),
            shape((BAND, TILE), BF16),
            shape((TILE, 2 * TILE), BF16),
            shape((2 * TILE, 2 * TILE), BF16),
        ),
        in_specs=[HBM] * 4,
        out_specs=(VMEM,) * 5,
        scratch_shapes=[
            pltpu.SMEM((2, 4), jnp.int32),
            pltpu.VMEM((4, TILE, TILE), BF16),
            pltpu.VMEM((4, TILE, TILE), F32),
            pltpu.VMEM((2 * TILE, TILE), BF16),
            pltpu.SemaphoreType.DMA((4,)),
        ],
        compiler_params=pltpu.CompilerParams(vmem_limit_bytes=16 * 1024 * 1024),
        name="bands",
    )(*[pltpu.with_memory_space_constraint(a, pltpu.HBM) for a in (band_offsets.T, g, m, down)])
    got = lax.all_to_all(jnp.broadcast_to(packed[None], (16, 8, TILE)), "z", 0, 0, axis_index_groups=[[(z + 8) % 16 for z in range(16)]])
    blocks = pl.pallas_call(
        block_kernel,
        out_shape=shape((16, ROWS, TILE), BF16),
        in_specs=[VMEM] * 3,
        out_specs=VMEM,
        compiler_params=PARAMS,
        name="blocks",
    )(got, params, freq)
    own = lax.all_to_all(blocks, PLANE, 0, 0, axis_index_groups=[list(range(15, -1, -1))])
    other = lax.ppermute(own, "core", [(0, 1), (1, 0)])
    new_momentum, all_rows, all_cols = pl.pallas_call(
        momentum_kernel,
        out_shape=(
            shape((4, TILE, TILE), F32),
            shape((4, TILE, 2 * TILE), BF16),
            shape((4, TILE, 2 * TILE), BF16),
        ),
        in_specs=[VMEM] * 7,
        out_specs=(VMEM,) * 3,
        compiler_params=PARAMS,
        cost_estimate=pl.CostEstimate(flops=200_000_000, bytes_accessed=700_000, transcendentals=0),
        name="momentum",
    )(g, m, bands, rows, cols, own, down)
    whole = pl.pallas_call(
        update_kernel,
        out_shape=shape((32, TILE, TILE), BF16),
        in_specs=[VMEM] * 4,
        out_specs=HBM,
        scratch_shapes=[pltpu.VMEM((32, TILE, TILE), BF16), pltpu.SemaphoreType.DMA((4,))],
        compiler_params=PARAMS,
        name="update",
    )(own, other, all_rows, all_cols)
    return (new_momentum[None], whole)


def solution(mesh):
    fine = Mesh(mesh.devices.reshape(2, 16, 2, 4, 2), AXES)
    rep, shard = ("yh", "z", "core"), ("x", "yl")
    in_specs = (P(rep, shard, None, None), P(rep, shard, None, None), P(shard, None, None), P(shard, None))
    out_specs = (P(rep, shard, None, None), P())
    return jax.shard_map(per_device, mesh=fine, in_specs=in_specs, out_specs=out_specs, check_vma=False)
```

```python
import functools
import math

import jax
import jax.numpy as jnp
import numpy as np
from jax import lax
from jax.experimental import pallas as pl
from jax.experimental.pallas import tpu as pltpu
from jax.sharding import Mesh, PartitionSpec as P

BAND = 16
TILE = 128
AXES = ("yh", "z", "core", "x", "yl")
PLANE = ("yh", "yl", "x")
F32 = jnp.float32
BF16 = jnp.bfloat16
Z_ORDER = [(z + 9) % 16 for z in range(16)]
PLANE_ORDER = [10] + [i for i in range(15, -1, -1) if i != 10]
ROWS = 160


def cosine_table():
    k = np.arange(TILE, dtype=np.float64)[:, None]
    x = np.arange(TILE, dtype=np.float64)[None, :]
    factor = np.where(k == 0, math.sqrt(1.0 / TILE), math.sqrt(2.0 / TILE))
    return factor * np.cos(math.pi * (x + 0.5) * k / TILE)


def split_table():
    table = cosine_table().astype(np.float32)
    high = table.astype(jnp.bfloat16)
    low = (table - high.astype(np.float32)).astype(jnp.bfloat16)
    return np.concatenate([high.T, low.T], axis=0)


def iota(shape, dim):
    return lax.broadcasted_iota(jnp.int32, shape, dim)


def dot(a, b):
    return lax.dot_general(a, b, (((1,), (0,)), ((), ())), preferred_element_type=F32)


def dot_nt(a, b):
    return lax.dot_general(a, b, (((1,), (1,)), ((), ())), preferred_element_type=F32)


def pieces(v):
    high = v.astype(BF16)
    low = (v - high.astype(F32)).astype(BF16)
    return high, low


def fold(v):
    return v[:, :TILE] + v[:, TILE:]


def wide(v):
    high, low = pieces(v)
    return jnp.concatenate([high, low], axis=1)


def weights(v):
    both = wide(v)
    return jnp.concatenate([both, both], axis=0)


def frequencies(offs_ref, which):
    lane = iota((1, TILE), 1)
    tile = (lane % 64) // BAND
    freq = lane % BAND
    for t in range(4):
        freq = freq + jnp.where(tile == t, offs_ref[which, t], 0)
    return freq


def tables(freq, down):
    picks = (iota((TILE, TILE), 0) == freq).astype(F32).astype(BF16)
    both = dot(down, picks)
    return both[:TILE].astype(BF16), both[TILE:].astype(BF16)


def masks(count, dtype):
    lanes = iota((1, 2 * TILE), 1)
    return [((lanes % TILE) // BAND == t).astype(F32).astype(dtype) for t in range(count)]


def stacked(high, low):
    return jnp.concatenate(
        [jnp.concatenate([high, high], axis=1), jnp.concatenate([low, low], axis=1)], axis=0
    )


def bands_kernel(
    offs_hbm, g_hbm, m_hbm, down_hbm, packed_ref, bands_ref, freq_ref, rows_ref, cols_ref, offs_ref, g_ref, m_ref, down_ref, sems
):
    copies = [
        pltpu.make_async_copy(src, dst, sems.at[i])
        for i, (src, dst) in enumerate(
            ((offs_hbm, offs_ref), (down_hbm, down_ref), (m_hbm, m_ref), (g_hbm, g_ref))
        )
    ]
    for copy in copies:
        copy.start()
    lane = iota((1, TILE), 1)
    slot = (lane % 64) // BAND
    copies[0].wait()
    row_freq, col_freq = frequencies(offs_ref, 0), frequencies(offs_ref, 1)
    steps = iota((BAND, TILE), 1) - iota((BAND, TILE), 0)
    picks = jnp.concatenate([(steps == offs_ref[0, t]).astype(F32) for t in range(4)], axis=0)
    copies[1].wait()
    down = down_ref[...]
    cols_high, cols_low = tables(col_freq, down)
    cols = jnp.concatenate([cols_high, cols_low], axis=1)
    cols_ref[...] = stacked(cols_high, cols_low)
    cols = jnp.concatenate([cols, cols], axis=0)
    rows = dot_nt(picks.astype(BF16), down).astype(BF16)
    rows_ref[...] = jnp.concatenate(tables(row_freq, down), axis=1)
    row = iota((BAND, TILE), 0)
    freq_ref[...] = jnp.where(row == 0, row_freq, col_freq).astype(F32).astype(BF16)
    copies[2].wait()
    copies[3].wait()
    right = jnp.zeros((TILE, TILE), F32)
    for t in range(4):
        moment = 0.9 * m_ref[t] + g_ref[t].astype(F32)
        right = jnp.where(slot == t, fold(dot(wide(moment), cols)), right)
    every = fold(dot(rows, weights(right)))
    bands = jnp.zeros((BAND, TILE), F32)
    for t in range(4):
        bands = jnp.where(slot == t, every[BAND * t : BAND * t + BAND], bands)
    bands_ref[...] = bands
    packed_ref[...] = jnp.where(lane < 64, bands[:8], bands[8:])


def block_kernel(got_ref, params_ref, freq_ref, out_ref):
    first = iota((1, TILE), 1) < 64
    total = jnp.sum(got_ref[...], axis=0)
    turned = pltpu.roll(total, 64, 1)
    high, low = [p.astype(F32) for p in pieces(total)]
    turned_high, turned_low = [p.astype(F32) for p in pieces(turned)]
    bands = jnp.concatenate(
        [jnp.where(first, high, turned_low), jnp.where(first, turned_high, low)], axis=0
    ).astype(BF16)
    block = params_ref[2 * lax.axis_index("core") + lax.axis_index("yh")]
    freq = freq_ref[...]
    for d in range(16):
        out_ref[d, :128] = block
        out_ref[d, 128:144] = bands
        out_ref[d, 144:] = freq


def source(yh, s):
    return PLANE_ORDER.index(8 * yh + 4 * (s % 2) + s // 2)


def momentum_kernel(g_ref, m_ref, bands_ref, rows_ref, cols_ref, got_ref, down_ref, out_ref, all_rows_ref, all_cols_ref):
    lane = iota((1, TILE), 1)
    bands = bands_ref[...]
    diagonal = [jnp.where(lane // BAND == t, bands, 0.0) for t in range(4)]
    diagonal = jnp.concatenate(diagonal + [jnp.zeros((64, TILE), F32)], axis=0)
    half = wide(fold(dot(rows_ref[...], weights(diagonal))))
    cols = cols_ref[...]
    for t, mask in enumerate(masks(4, BF16)):
        moment = 0.9 * m_ref[t] + g_ref[t].astype(F32)
        out_ref[t] = moment - fold(dot_nt(half * mask, cols))
    down = down_ref[...]
    for g in range(4):
        freqs = [got_ref[source(0, s), 144:160].astype(F32).astype(jnp.int32) for s in (2 * g, 2 * g + 1)]
        freqs = jnp.where(lane < 64, freqs[0], freqs[1])
        all_rows_ref[g] = jnp.concatenate(tables(freqs[0:1], down), axis=1)
        picks = (iota((TILE, TILE), 0) == freqs[1:2]).astype(F32).T.astype(BF16)
        all_cols_ref[g] = dot_nt(picks, down).astype(BF16)


def update_kernel(own_ref, other_ref, rows_ref, cols_ref, out_hbm, out_ref, sems):
    lane = iota((1, TILE), 1)
    first = lane < 64
    core = lax.axis_index("core")
    halves = []
    squares = []
    for g in range(4):
        sums = []
        for s in (2 * g, 2 * g + 1):
            v = sum(ref[source(yh, s), 128:144].astype(F32) for ref in (own_ref, other_ref) for yh in range(2))
            sums.append((v + pltpu.roll(v, 64, 1)) * (1.0 / 64))
        both = jnp.where(first, sums[0], sums[1])
        squares.append(jnp.sum(both * both, axis=0, keepdims=True))
        diagonal = jnp.concatenate([jnp.where(lane // BAND == t, sums[t // 4], 0.0) for t in range(8)], axis=0)
        halves.append(fold(dot(rows_ref[g], weights(diagonal))))
    squares = jnp.concatenate(squares + squares, axis=0)
    same = (iota((TILE, TILE), 0) // BAND == iota((TILE, TILE), 1) // BAND).astype(F32).astype(BF16)
    high, low = pieces(squares)
    mean = (dot(high, same) + dot(low, same)) * (1.0 / (TILE * TILE))
    inverse = 1.0 / jnp.sqrt(mean + 1e-06)
    lanes = (iota((1, 2 * TILE), 1) % TILE) // BAND
    order = [(ref, half_of, sh, yh) for sh in range(2) for ref, half_of in ((own_ref, core), (other_ref, 1 - core)) for yh in range(2)]
    copies = []
    for g in range(4):
        half = wide(halves[g] * inverse[g : g + 1])
        left = jnp.concatenate(
            [half * (lanes == 4 * sh + 2 * half_of + yh).astype(F32).astype(BF16) for _, half_of, sh, yh in order], axis=0
        )
        cols = cols_ref[g]
        update = fold(dot(left, jnp.concatenate([cols, cols], axis=0)))
        for i, (ref, half_of, sh, yh) in enumerate(order):
            s = 2 * g + sh
            params = ref[source(yh, s), :128].astype(F32)
            out_ref[4 * s + 2 * half_of + yh] = (params - update[TILE * i : TILE * i + TILE]).astype(BF16)
            if i % 4 == 3:
                tiles = pl.ds(4 * s, 4)
                copies.append(pltpu.make_async_copy(out_ref.at[tiles], out_hbm.at[tiles], sems.at[s]))
                copies[-1].start()
    for copy in copies:
        copy.wait()


SMEM = pl.BlockSpec(memory_space=pltpu.SMEM)
VMEM = pl.BlockSpec(memory_space=pltpu.VMEM)
HBM = pl.BlockSpec(memory_space=pltpu.HBM)
PARAMS = pltpu.CompilerParams(vmem_limit_bytes=40 * 1024 * 1024)
shape = jax.ShapeDtypeStruct


def per_device(gradients, momentum, params, band_offsets):
    down = jnp.asarray(split_table())
    g, m = gradients[0], momentum[0]
    packed, bands, freq, rows, cols = pl.pallas_call(
        bands_kernel,
        out_shape=(
            shape((8, TILE), F32),
            shape((BAND, TILE), F32),
            shape((BAND, TILE), BF16),
            shape((TILE, 2 * TILE), BF16),
            shape((2 * TILE, 2 * TILE), BF16),
        ),
        in_specs=[HBM] * 4,
        out_specs=(VMEM,) * 5,
        scratch_shapes=[
            pltpu.SMEM((2, 4), jnp.int32),
            pltpu.VMEM((4, TILE, TILE), BF16),
            pltpu.VMEM((4, TILE, TILE), F32),
            pltpu.VMEM((2 * TILE, TILE), BF16),
            pltpu.SemaphoreType.DMA((4,)),
        ],
        compiler_params=pltpu.CompilerParams(vmem_limit_bytes=16 * 1024 * 1024),
        name="bands",
    )(*[pltpu.with_memory_space_constraint(a, pltpu.HBM) for a in (band_offsets.T, g, m, down)])
    got = lax.all_to_all(jnp.broadcast_to(packed[None], (16, 8, TILE)), "z", 0, 0, axis_index_groups=[Z_ORDER])
    blocks = pl.pallas_call(
        block_kernel,
        out_shape=shape((16, ROWS, TILE), BF16),
        in_specs=[VMEM] * 3,
        out_specs=VMEM,
        compiler_params=PARAMS,
        name="blocks",
    )(got, params, freq)
    own = lax.all_to_all(blocks, PLANE, 0, 0, axis_index_groups=[PLANE_ORDER])
    other = lax.ppermute(own, "core", [(0, 1), (1, 0)])
    new_momentum, all_rows, all_cols = pl.pallas_call(
        momentum_kernel,
        out_shape=(
            shape((4, TILE, TILE), F32),
            shape((4, TILE, 2 * TILE), BF16),
            shape((4, TILE, 2 * TILE), BF16),
        ),
        in_specs=[VMEM] * 7,
        out_specs=(VMEM,) * 3,
        compiler_params=PARAMS,
        cost_estimate=pl.CostEstimate(flops=200_000_000, bytes_accessed=700_000, transcendentals=0),
        name="momentum",
    )(g, m, bands, rows, cols, own, down)
    whole = pl.pallas_call(
        update_kernel,
        out_shape=shape((32, TILE, TILE), BF16),
        in_specs=[VMEM] * 4,
        out_specs=HBM,
        scratch_shapes=[pltpu.VMEM((32, TILE, TILE), BF16), pltpu.SemaphoreType.DMA((8,))],
        compiler_params=PARAMS,
        name="update",
    )(own, other, all_rows, all_cols)
    return (new_momentum[None], whole)


def solution(mesh):
    fine = Mesh(mesh.devices.reshape(2, 16, 2, 4, 2), AXES)
    rep, shard = ("yh", "z", "core"), ("x", "yl")
    in_specs = (P(rep, shard, None, None), P(rep, shard, None, None), P(shard, None, None), P(shard, None))
    out_specs = (P(rep, shard, None, None), P())
    return jax.shard_map(per_device, mesh=fine, in_specs=in_specs, out_specs=out_specs, check_vma=False)
```

```python
import functools
import math

import jax
import jax.numpy as jnp
import numpy as np
from jax import lax
from jax.experimental import pallas as pl
from jax.experimental.pallas import tpu as pltpu
from jax.sharding import Mesh, PartitionSpec as P

BAND = 16
TILE = 128
AXES = ("yh", "z", "core", "x", "yl")
PLANE = ("yh", "yl", "x")
F32 = jnp.float32
BF16 = jnp.bfloat16
Z_ORDER = [8, 0, 1, 15, 2, 14, 3, 13, 4, 12, 5, 11, 6, 10, 7, 9]
PLANE_ORDER = [10] + [i for i in range(15, -1, -1) if i != 10]
ROWS = 160


def cosine_table():
    k = np.arange(TILE, dtype=np.float64)[:, None]
    x = np.arange(TILE, dtype=np.float64)[None, :]
    factor = np.where(k == 0, math.sqrt(1.0 / TILE), math.sqrt(2.0 / TILE))
    return factor * np.cos(math.pi * (x + 0.5) * k / TILE)


def split_table():
    table = cosine_table().astype(np.float32)
    high = table.astype(jnp.bfloat16)
    low = (table - high.astype(np.float32)).astype(jnp.bfloat16)
    return np.concatenate([high.T, low.T], axis=0)


def iota(shape, dim):
    return lax.broadcasted_iota(jnp.int32, shape, dim)


def dot(a, b):
    return lax.dot_general(a, b, (((1,), (0,)), ((), ())), preferred_element_type=F32)


def dot_nt(a, b):
    return lax.dot_general(a, b, (((1,), (1,)), ((), ())), preferred_element_type=F32)


def pieces(v):
    high = v.astype(BF16)
    low = (v - high.astype(F32)).astype(BF16)
    return high, low


def fold(v):
    return v[:, :TILE] + v[:, TILE:]


def wide(v):
    high, low = pieces(v)
    return jnp.concatenate([high, low], axis=1)


def weights(v):
    both = wide(v)
    return jnp.concatenate([both, both], axis=0)


def frequencies(offs_ref, which):
    lane = iota((1, TILE), 1)
    tile = (lane % 64) // BAND
    freq = lane % BAND
    for t in range(4):
        freq = freq + jnp.where(tile == t, offs_ref[which, t], 0)
    return freq


def tables(freq, down):
    picks = (iota((TILE, TILE), 0) == freq).astype(F32).astype(BF16)
    both = dot(down, picks)
    return both[:TILE].astype(BF16), both[TILE:].astype(BF16)


def masks(count, dtype):
    lanes = iota((1, 2 * TILE), 1)
    return [((lanes % TILE) // BAND == t).astype(F32).astype(dtype) for t in range(count)]


def stacked(high, low):
    return jnp.concatenate(
        [jnp.concatenate([high, high], axis=1), jnp.concatenate([low, low], axis=1)], axis=0
    )


def bands_kernel(
    offs_hbm, g_hbm, m_hbm, down_hbm, packed_ref, bands_ref, freq_ref, offs_ref, g_ref, m_ref, down_ref, sems
):
    copies = [
        pltpu.make_async_copy(src, dst, sems.at[i])
        for i, (src, dst) in enumerate(
            ((offs_hbm, offs_ref), (down_hbm, down_ref), (m_hbm, m_ref), (g_hbm, g_ref))
        )
    ]
    for copy in copies:
        copy.start()
    lane = iota((1, TILE), 1)
    slot = (lane % 64) // BAND
    copies[0].wait()
    row_freq, col_freq = frequencies(offs_ref, 0), frequencies(offs_ref, 1)
    steps = iota((BAND, TILE), 1) - iota((BAND, TILE), 0)
    picks = jnp.concatenate([(steps == offs_ref[0, t]).astype(F32) for t in range(4)], axis=0)
    copies[1].wait()
    down = down_ref[...]
    cols_high, cols_low = tables(col_freq, down)
    cols = jnp.concatenate([cols_high, cols_low], axis=1)
    cols = jnp.concatenate([cols, cols], axis=0)
    rows = dot_nt(picks.astype(BF16), down).astype(BF16)
    row = iota((BAND, TILE), 0)
    freq_ref[...] = jnp.where(row == 0, row_freq, col_freq).astype(F32).astype(BF16)
    copies[2].wait()
    copies[3].wait()
    right = jnp.zeros((TILE, TILE), F32)
    for t in range(4):
        moment = 0.9 * m_ref[t] + g_ref[t].astype(F32)
        right = jnp.where(slot == t, fold(dot(wide(moment), cols)), right)
    every = fold(dot(rows, weights(right)))
    bands = jnp.zeros((BAND, TILE), F32)
    for t in range(4):
        bands = jnp.where(slot == t, every[BAND * t : BAND * t + BAND], bands)
    bands_ref[...] = bands
    packed_ref[...] = jnp.where(lane < 64, bands[:8], bands[8:])


def block_kernel(got_ref, params_ref, freq_ref, out_ref):
    first = iota((1, TILE), 1) < 64
    total = jnp.sum(got_ref[...], axis=0)
    turned = pltpu.roll(total, 64, 1)
    high, low = [p.astype(F32) for p in pieces(total)]
    turned_high, turned_low = [p.astype(F32) for p in pieces(turned)]
    bands = jnp.concatenate(
        [jnp.where(first, high, turned_low), jnp.where(first, turned_high, low)], axis=0
    ).astype(BF16)
    block = params_ref[2 * lax.axis_index("core") + lax.axis_index("yh")]
    freq = freq_ref[...]
    for d in range(16):
        out_ref[d, :128] = block
        out_ref[d, 128:144] = bands
        out_ref[d, 144:] = freq


def source(yh, s):
    return PLANE_ORDER.index(8 * yh + 4 * (s % 2) + s // 2)


def momentum_kernel(g_ref, m_ref, bands_ref, freq_ref, got_ref, down_ref, out_ref, all_rows_ref, all_cols_ref):
    lane = iota((1, TILE), 1)
    bands = bands_ref[...]
    diagonal = [jnp.where(lane // BAND == t, bands, 0.0) for t in range(4)]
    diagonal = jnp.concatenate(diagonal + [jnp.zeros((64, TILE), F32)], axis=0)
    down = down_ref[...]
    own = freq_ref[...].astype(F32).astype(jnp.int32)
    half = wide(fold(dot(jnp.concatenate(tables(own[0:1], down), axis=1), weights(diagonal))))
    cols = stacked(*tables(own[1:2], down))
    for t, mask in enumerate(masks(4, BF16)):
        moment = 0.9 * m_ref[t] + g_ref[t].astype(F32)
        out_ref[t] = moment - fold(dot_nt(half * mask, cols))
    for g in range(4):
        freqs = [got_ref[source(0, s), 144:160].astype(F32).astype(jnp.int32) for s in (2 * g, 2 * g + 1)]
        freqs = jnp.where(lane < 64, freqs[0], freqs[1])
        all_rows_ref[g] = jnp.concatenate(tables(freqs[0:1], down), axis=1)
        picks = (iota((TILE, TILE), 0) == freqs[1:2]).astype(F32).T.astype(BF16)
        all_cols_ref[g] = dot_nt(picks, down).astype(BF16)


def update_kernel(own_ref, other_ref, rows_ref, cols_ref, out_hbm, out_ref, sems):
    lane = iota((1, TILE), 1)
    first = lane < 64
    core = lax.axis_index("core")
    halves = []
    squares = []
    for g in range(4):
        sums = []
        for s in (2 * g, 2 * g + 1):
            v = sum(ref[source(yh, s), 128:144].astype(F32) for ref in (own_ref, other_ref) for yh in range(2))
            sums.append((v + pltpu.roll(v, 64, 1)) * (1.0 / 64))
        both = jnp.where(first, sums[0], sums[1])
        squares.append(jnp.sum(both * both, axis=0, keepdims=True))
        diagonal = jnp.concatenate([jnp.where(lane // BAND == t, sums[t // 4], 0.0) for t in range(8)], axis=0)
        halves.append(fold(dot(rows_ref[g], weights(diagonal))))
    squares = jnp.concatenate(squares + squares, axis=0)
    same = (iota((TILE, TILE), 0) // BAND == iota((TILE, TILE), 1) // BAND).astype(F32).astype(BF16)
    high, low = pieces(squares)
    mean = (dot(high, same) + dot(low, same)) * (1.0 / (TILE * TILE))
    inverse = 1.0 / jnp.sqrt(mean + 1e-06)
    lanes = (iota((1, 2 * TILE), 1) % TILE) // BAND
    order = [(ref, half_of, sh, yh) for sh in range(2) for ref, half_of in ((own_ref, core), (other_ref, 1 - core)) for yh in range(2)]
    copies = []
    for g in range(4):
        half = wide(halves[g] * inverse[g : g + 1])
        left = jnp.concatenate(
            [half * (lanes == 4 * sh + 2 * half_of + yh).astype(F32).astype(BF16) for _, half_of, sh, yh in order], axis=0
        )
        cols = cols_ref[g]
        update = fold(dot(left, jnp.concatenate([cols, cols], axis=0)))
        for i, (ref, half_of, sh, yh) in enumerate(order):
            s = 2 * g + sh
            params = ref[source(yh, s), :128].astype(F32)
            out_ref[4 * s + 2 * half_of + yh] = (params - update[TILE * i : TILE * i + TILE]).astype(BF16)
            if i % 4 == 3:
                tiles = pl.ds(4 * s, 4)
                copies.append(pltpu.make_async_copy(out_ref.at[tiles], out_hbm.at[tiles], sems.at[s]))
                copies[-1].start()
    for copy in copies:
        copy.wait()


SMEM = pl.BlockSpec(memory_space=pltpu.SMEM)
VMEM = pl.BlockSpec(memory_space=pltpu.VMEM)
HBM = pl.BlockSpec(memory_space=pltpu.HBM)
PARAMS = pltpu.CompilerParams(vmem_limit_bytes=40 * 1024 * 1024)
shape = jax.ShapeDtypeStruct


def per_device(gradients, momentum, params, band_offsets):
    down = jnp.asarray(split_table())
    g, m = gradients[0], momentum[0]
    packed, bands, freq = pl.pallas_call(
        bands_kernel,
        out_shape=(
            shape((8, TILE), F32),
            shape((BAND, TILE), F32),
            shape((BAND, TILE), BF16),
        ),
        in_specs=[HBM] * 4,
        out_specs=(VMEM,) * 3,
        scratch_shapes=[
            pltpu.SMEM((2, 4), jnp.int32),
            pltpu.VMEM((4, TILE, TILE), BF16),
            pltpu.VMEM((4, TILE, TILE), F32),
            pltpu.VMEM((2 * TILE, TILE), BF16),
            pltpu.SemaphoreType.DMA((4,)),
        ],
        compiler_params=pltpu.CompilerParams(vmem_limit_bytes=16 * 1024 * 1024),
        name="bands",
    )(*[pltpu.with_memory_space_constraint(a, pltpu.HBM) for a in (band_offsets.T, g, m, down)])
    got = lax.all_to_all(jnp.broadcast_to(packed[None], (16, 8, TILE)), "z", 0, 0, axis_index_groups=[Z_ORDER])
    blocks = pl.pallas_call(
        block_kernel,
        out_shape=shape((16, ROWS, TILE), BF16),
        in_specs=[VMEM] * 3,
        out_specs=VMEM,
        compiler_params=PARAMS,
        name="blocks",
    )(got, params, freq)
    own = lax.all_to_all(blocks, PLANE, 0, 0, axis_index_groups=[PLANE_ORDER])
    other = lax.ppermute(own, "core", [(0, 1), (1, 0)])
    new_momentum, all_rows, all_cols = pl.pallas_call(
        momentum_kernel,
        out_shape=(
            shape((4, TILE, TILE), F32),
            shape((4, TILE, 2 * TILE), BF16),
            shape((4, TILE, 2 * TILE), BF16),
        ),
        in_specs=[VMEM] * 6,
        out_specs=(VMEM,) * 3,
        compiler_params=PARAMS,
        cost_estimate=pl.CostEstimate(flops=200_000_000, bytes_accessed=700_000, transcendentals=0),
        name="momentum",
    )(g, m, bands, freq, own, down)
    whole = pl.pallas_call(
        update_kernel,
        out_shape=shape((32, TILE, TILE), BF16),
        in_specs=[VMEM] * 4,
        out_specs=HBM,
        scratch_shapes=[pltpu.VMEM((32, TILE, TILE), BF16), pltpu.SemaphoreType.DMA((8,))],
        compiler_params=PARAMS,
        name="update",
    )(own, other, all_rows, all_cols)
    return (new_momentum[None], whole)


def solution(mesh):
    fine = Mesh(mesh.devices.reshape(2, 16, 2, 4, 2), AXES)
    rep, shard = ("yh", "z", "core"), ("x", "yl")
    in_specs = (P(rep, shard, None, None), P(rep, shard, None, None), P(shard, None, None), P(shard, None))
    out_specs = (P(rep, shard, None, None), P())
    return jax.shard_map(per_device, mesh=fine, in_specs=in_specs, out_specs=out_specs, check_vma=False)
```

```python
import functools
import math

import jax
import jax.numpy as jnp
import numpy as np
from jax import lax
from jax.experimental import pallas as pl
from jax.experimental.pallas import tpu as pltpu
from jax.sharding import Mesh, PartitionSpec as P

BAND = 16
TILE = 128
AXES = ("yh", "z", "core", "x", "yl")
PLANE = ("yh", "yl", "x")
F32 = jnp.float32
BF16 = jnp.bfloat16
Z_ORDER = [8, 0, 1, 15, 2, 14, 3, 13, 4, 12, 5, 11, 6, 10, 7, 9]
PLANE_ORDER = [10] + [i for i in range(15, -1, -1) if i != 10]
ROWS = 160


def cosine_table():
    k = np.arange(TILE, dtype=np.float64)[:, None]
    x = np.arange(TILE, dtype=np.float64)[None, :]
    factor = np.where(k == 0, math.sqrt(1.0 / TILE), math.sqrt(2.0 / TILE))
    return factor * np.cos(math.pi * (x + 0.5) * k / TILE)


def split_table():
    table = cosine_table().astype(np.float32)
    high = table.astype(jnp.bfloat16)
    low = (table - high.astype(np.float32)).astype(jnp.bfloat16)
    return np.concatenate([high.T, low.T], axis=0)


def iota(shape, dim):
    return lax.broadcasted_iota(jnp.int32, shape, dim)


def dot(a, b):
    return lax.dot_general(a, b, (((1,), (0,)), ((), ())), preferred_element_type=F32)


def dot_nt(a, b):
    return lax.dot_general(a, b, (((1,), (1,)), ((), ())), preferred_element_type=F32)


def pieces(v):
    high = v.astype(BF16)
    low = (v - high.astype(F32)).astype(BF16)
    return high, low


def fold(v):
    return v[:, :TILE] + v[:, TILE:]


def wide(v):
    high, low = pieces(v)
    return jnp.concatenate([high, low], axis=1)


def weights(v):
    both = wide(v)
    return jnp.concatenate([both, both], axis=0)


def frequencies(offs_ref, which):
    lane = iota((1, TILE), 1)
    tile = (lane % 64) // BAND
    freq = lane % BAND
    for t in range(4):
        freq = freq + jnp.where(tile == t, offs_ref[which, t], 0)
    return freq


def tables(freq, down):
    picks = (iota((TILE, TILE), 0) == freq).astype(F32).astype(BF16)
    both = dot(down, picks)
    return both[:TILE].astype(BF16), both[TILE:].astype(BF16)


def masks(count, dtype):
    lanes = iota((1, 2 * TILE), 1)
    return [((lanes % TILE) // BAND == t).astype(F32).astype(dtype) for t in range(count)]


def stacked(high, low):
    return jnp.concatenate(
        [jnp.concatenate([high, high], axis=1), jnp.concatenate([low, low], axis=1)], axis=0
    )


def bands_kernel(
    offs_hbm, g_hbm, m_hbm, down_hbm, packed_ref, bands_ref, freq_ref, offs_ref, g_ref, m_ref, down_ref, sems
):
    copies = [
        pltpu.make_async_copy(src, dst, sems.at[i])
        for i, (src, dst) in enumerate(
            ((offs_hbm, offs_ref), (down_hbm, down_ref), (m_hbm, m_ref), (g_hbm, g_ref))
        )
    ]
    for copy in copies:
        copy.start()
    lane = iota((1, TILE), 1)
    slot = (lane % 64) // BAND
    copies[0].wait()
    row_freq, col_freq = frequencies(offs_ref, 0), frequencies(offs_ref, 1)
    steps = iota((BAND, TILE), 1) - iota((BAND, TILE), 0)
    picks = jnp.concatenate([(steps == offs_ref[0, t]).astype(F32) for t in range(4)], axis=0)
    copies[1].wait()
    down = down_ref[...]
    cols_high, cols_low = tables(col_freq, down)
    cols = jnp.concatenate([cols_high, cols_low], axis=1)
    cols = jnp.concatenate([cols, cols], axis=0)
    rows = dot_nt(picks.astype(BF16), down).astype(BF16)
    row = iota((BAND, TILE), 0)
    freq_ref[...] = jnp.where(row == 0, row_freq, col_freq).astype(F32).astype(BF16)
    copies[2].wait()
    copies[3].wait()
    right = jnp.zeros((TILE, TILE), F32)
    for t in range(4):
        moment = 0.9 * m_ref[t] + g_ref[t].astype(F32)
        right = jnp.where(slot == t, fold(dot(wide(moment), cols)), right)
    every = fold(dot(rows, weights(right)))
    bands = jnp.zeros((BAND, TILE), F32)
    for t in range(4):
        bands = jnp.where(slot == t, every[BAND * t : BAND * t + BAND], bands)
    bands_ref[...] = bands
    packed_ref[...] = jnp.where(lane < 64, bands[:8], bands[8:])


def block_kernel(got_ref, params_ref, freq_ref, out_ref):
    first = iota((1, TILE), 1) < 64
    total = jnp.sum(got_ref[...], axis=0)
    turned = pltpu.roll(total, 64, 1)
    high, low = [p.astype(F32) for p in pieces(total)]
    turned_high, turned_low = [p.astype(F32) for p in pieces(turned)]
    bands = jnp.concatenate(
        [jnp.where(first, high, turned_low), jnp.where(first, turned_high, low)], axis=0
    ).astype(BF16)
    block = params_ref[2 * lax.axis_index("core") + lax.axis_index("yh")]
    freq = freq_ref[...]
    for d in range(16):
        out_ref[d, :128] = block
        out_ref[d, 128:144] = bands
        out_ref[d, 144:] = freq


def source(yh, s):
    return PLANE_ORDER.index(8 * yh + 4 * (s % 2) + s // 2)


def momentum_kernel(g_ref, m_ref, bands_ref, freq_ref, got_ref, down_ref, out_ref, all_rows_ref, all_cols_ref):
    lane = iota((1, TILE), 1)
    bands = bands_ref[...]
    diagonal = [jnp.where(lane // BAND == t, bands, 0.0) for t in range(4)]
    diagonal = jnp.concatenate(diagonal + [jnp.zeros((64, TILE), F32)], axis=0)
    down = down_ref[...]
    own = freq_ref[...].astype(F32).astype(jnp.int32)
    half = wide(fold(dot(jnp.concatenate(tables(own[0:1], down), axis=1), weights(diagonal))))
    cols = stacked(*tables(own[1:2], down))
    for t, mask in enumerate(masks(4, BF16)):
        moment = 0.9 * m_ref[t] + g_ref[t].astype(F32)
        out_ref[t] = moment - fold(dot_nt(half * mask, cols))
    for g in range(4):
        freqs = [got_ref[source(0, s), 144:160].astype(F32).astype(jnp.int32) for s in (2 * g, 2 * g + 1)]
        freqs = jnp.where(lane < 64, freqs[0], freqs[1])
        all_rows_ref[g] = jnp.concatenate(tables(freqs[0:1], down), axis=1)
        picks = (iota((TILE, TILE), 0) == freqs[1:2]).astype(F32).T.astype(BF16)
        both = dot_nt(picks, down)
        odd = (iota((TILE, TILE), 0) // BAND) % 2 == 1
        for sh in range(2):
            parts = []
            for part in (both[:, :TILE], both[:, TILE:]):
                spread = jnp.concatenate([jnp.where(odd, 0.0, part), jnp.where(odd, part, 0.0)], axis=1)
                parts += [spread[64 * sh : 64 * sh + 64]] * 2
            all_cols_ref[2 * g + sh] = jnp.concatenate(parts, axis=0).astype(BF16)


def update_kernel(own_ref, other_ref, rows_ref, cols_ref, out_hbm, out_ref, sems):
    lane = iota((1, TILE), 1)
    first = lane < 64
    core = lax.axis_index("core")
    halves = []
    squares = []
    for g in range(4):
        sums = []
        for s in (2 * g, 2 * g + 1):
            v = sum(ref[source(yh, s), 128:144].astype(F32) for ref in (own_ref, other_ref) for yh in range(2))
            sums.append((v + pltpu.roll(v, 64, 1)) * (1.0 / 64))
        both = jnp.where(first, sums[0], sums[1])
        squares.append(jnp.sum(both * both, axis=0, keepdims=True))
        diagonal = jnp.concatenate([jnp.where(lane // BAND == t, sums[t // 4], 0.0) for t in range(8)], axis=0)
        halves.append(fold(dot(rows_ref[g], weights(diagonal))))
    squares = jnp.concatenate(squares + squares, axis=0)
    same = (iota((TILE, TILE), 0) // BAND == iota((TILE, TILE), 1) // BAND).astype(F32).astype(BF16)
    high, low = pieces(squares)
    mean = (dot(high, same) + dot(low, same)) * (1.0 / (TILE * TILE))
    inverse = 1.0 / jnp.sqrt(mean + 1e-06)
    pair = (iota((1, 2 * TILE), 1) % 64) // (2 * BAND)
    order = ((own_ref, core), (other_ref, 1 - core))
    copies = []
    for g in range(4):
        high, low = [p.astype(F32) for p in pieces(halves[g] * inverse[g : g + 1])]
        for sh in range(2):
            s = 2 * g + sh
            if sh == 0:
                half = jnp.where(first, high, pltpu.roll(low, 64, 1)).astype(BF16)
            else:
                half = jnp.where(first, pltpu.roll(high, 64, 1), low).astype(BF16)
            half = jnp.concatenate([half, half], axis=1)
            left = jnp.concatenate([half * (pair == half_of).astype(F32).astype(BF16) for _, half_of in order], axis=0)
            update = dot(left, cols_ref[s])
            for i, (ref, half_of) in enumerate(order):
                for yh in range(2):
                    params = ref[source(yh, s), :128].astype(F32)
                    own = update[TILE * i : TILE * i + TILE, TILE * yh : TILE * yh + TILE]
                    out_ref[4 * s + 2 * half_of + yh] = (params - own).astype(BF16)
            tiles = pl.ds(4 * s, 4)
            copies.append(pltpu.make_async_copy(out_ref.at[tiles], out_hbm.at[tiles], sems.at[s]))
            copies[-1].start()
    for copy in copies:
        copy.wait()


SMEM = pl.BlockSpec(memory_space=pltpu.SMEM)
VMEM = pl.BlockSpec(memory_space=pltpu.VMEM)
HBM = pl.BlockSpec(memory_space=pltpu.HBM)
PARAMS = pltpu.CompilerParams(vmem_limit_bytes=40 * 1024 * 1024)
shape = jax.ShapeDtypeStruct


def per_device(gradients, momentum, params, band_offsets):
    down = jnp.asarray(split_table())
    g, m = gradients[0], momentum[0]
    packed, bands, freq = pl.pallas_call(
        bands_kernel,
        out_shape=(
            shape((8, TILE), F32),
            shape((BAND, TILE), F32),
            shape((BAND, TILE), BF16),
        ),
        in_specs=[HBM] * 4,
        out_specs=(VMEM,) * 3,
        scratch_shapes=[
            pltpu.SMEM((2, 4), jnp.int32),
            pltpu.VMEM((4, TILE, TILE), BF16),
            pltpu.VMEM((4, TILE, TILE), F32),
            pltpu.VMEM((2 * TILE, TILE), BF16),
            pltpu.SemaphoreType.DMA((4,)),
        ],
        compiler_params=pltpu.CompilerParams(vmem_limit_bytes=16 * 1024 * 1024),
        name="bands",
    )(*[pltpu.with_memory_space_constraint(a, pltpu.HBM) for a in (band_offsets.T, g, m, down)])
    got = lax.all_to_all(jnp.broadcast_to(packed[None], (16, 8, TILE)), "z", 0, 0, axis_index_groups=[Z_ORDER])
    blocks = pl.pallas_call(
        block_kernel,
        out_shape=shape((16, ROWS, TILE), BF16),
        in_specs=[VMEM] * 3,
        out_specs=VMEM,
        compiler_params=PARAMS,
        name="blocks",
    )(got, params, freq)
    own = lax.all_to_all(blocks, PLANE, 0, 0, axis_index_groups=[PLANE_ORDER])
    other = lax.ppermute(own, "core", [(0, 1), (1, 0)])
    new_momentum, all_rows, all_cols = pl.pallas_call(
        momentum_kernel,
        out_shape=(
            shape((4, TILE, TILE), F32),
            shape((4, TILE, 2 * TILE), BF16),
            shape((8, 2 * TILE, 2 * TILE), BF16),
        ),
        in_specs=[VMEM] * 6,
        out_specs=(VMEM,) * 3,
        compiler_params=PARAMS,
        cost_estimate=pl.CostEstimate(flops=200_000_000, bytes_accessed=700_000, transcendentals=0),
        name="momentum",
    )(g, m, bands, freq, own, down)
    whole = pl.pallas_call(
        update_kernel,
        out_shape=shape((32, TILE, TILE), BF16),
        in_specs=[VMEM] * 4,
        out_specs=HBM,
        scratch_shapes=[pltpu.VMEM((32, TILE, TILE), BF16), pltpu.SemaphoreType.DMA((8,))],
        compiler_params=PARAMS,
        name="update",
    )(own, other, all_rows, all_cols)
    return (new_momentum[None], whole)


def solution(mesh):
    fine = Mesh(mesh.devices.reshape(2, 16, 2, 4, 2), AXES)
    rep, shard = ("yh", "z", "core"), ("x", "yl")
    in_specs = (P(rep, shard, None, None), P(rep, shard, None, None), P(shard, None, None), P(shard, None))
    out_specs = (P(rep, shard, None, None), P())
    return jax.shard_map(per_device, mesh=fine, in_specs=in_specs, out_specs=out_specs, check_vma=False)
```

```python
import functools
import math

import jax
import jax.numpy as jnp
import numpy as np
from jax import lax
from jax.experimental import pallas as pl
from jax.experimental.pallas import tpu as pltpu
from jax.sharding import Mesh, PartitionSpec as P

BAND = 16
TILE = 128
AXES = ("yh", "z", "core", "x", "yl")
PLANE = ("yh", "yl", "x")
F32 = jnp.float32
BF16 = jnp.bfloat16
Z_ORDER = [8, 0, 1, 15, 2, 14, 3, 13, 4, 12, 5, 11, 6, 10, 7, 9]
PLANE_ORDER = [10] + [i for i in range(15, -1, -1) if i != 10]
ROWS = 160


def cosine_table():
    k = np.arange(TILE, dtype=np.float64)[:, None]
    x = np.arange(TILE, dtype=np.float64)[None, :]
    factor = np.where(k == 0, math.sqrt(1.0 / TILE), math.sqrt(2.0 / TILE))
    return factor * np.cos(math.pi * (x + 0.5) * k / TILE)


def split_table():
    table = cosine_table().astype(np.float32)
    high = table.astype(jnp.bfloat16)
    low = (table - high.astype(np.float32)).astype(jnp.bfloat16)
    return np.concatenate([high.T, low.T], axis=0)


def iota(shape, dim):
    return lax.broadcasted_iota(jnp.int32, shape, dim)


def dot(a, b):
    return lax.dot_general(a, b, (((1,), (0,)), ((), ())), preferred_element_type=F32)


def dot_nt(a, b):
    return lax.dot_general(a, b, (((1,), (1,)), ((), ())), preferred_element_type=F32)


def pieces(v):
    high = v.astype(BF16)
    low = (v - high.astype(F32)).astype(BF16)
    return high, low


def fold(v):
    return v[:, :TILE] + v[:, TILE:]


def wide(v):
    high, low = pieces(v)
    return jnp.concatenate([high, low], axis=1)


def weights(v):
    both = wide(v)
    return jnp.concatenate([both, both], axis=0)


def frequencies(offs_ref, which):
    lane = iota((1, TILE), 1)
    tile = (lane % 64) // BAND
    freq = lane % BAND
    for t in range(4):
        freq = freq + jnp.where(tile == t, offs_ref[which, t], 0)
    return freq


def tables(freq, down):
    picks = (iota((TILE, TILE), 0) == freq).astype(F32).astype(BF16)
    both = dot(down, picks)
    return both[:TILE].astype(BF16), both[TILE:].astype(BF16)


def masks(count, dtype):
    lanes = iota((1, 2 * TILE), 1)
    return [((lanes % TILE) // BAND == t).astype(F32).astype(dtype) for t in range(count)]


def stacked(high, low):
    return jnp.concatenate(
        [jnp.concatenate([high, high], axis=1), jnp.concatenate([low, low], axis=1)], axis=0
    )


def bands_kernel(
    offs_hbm, g_hbm, m_hbm, down_hbm, packed_ref, bands_ref, freq_ref, offs_ref, g_ref, m_ref, down_ref, sems
):
    copies = [
        pltpu.make_async_copy(src, dst, sems.at[i])
        for i, (src, dst) in enumerate(
            ((offs_hbm, offs_ref), (down_hbm, down_ref), (m_hbm, m_ref), (g_hbm, g_ref))
        )
    ]
    for copy in copies:
        copy.start()
    lane = iota((1, TILE), 1)
    slot = (lane % 64) // BAND
    copies[0].wait()
    row_freq, col_freq = frequencies(offs_ref, 0), frequencies(offs_ref, 1)
    steps = iota((BAND, TILE), 1) - iota((BAND, TILE), 0)
    picks = jnp.concatenate([(steps == offs_ref[0, t]).astype(F32) for t in range(4)], axis=0)
    copies[1].wait()
    down = down_ref[...]
    cols_high, cols_low = tables(col_freq, down)
    cols = jnp.concatenate([cols_high, cols_low], axis=1)
    cols = jnp.concatenate([cols, cols], axis=0)
    rows = dot_nt(picks.astype(BF16), down).astype(BF16)
    row = iota((BAND, TILE), 0)
    freq_ref[...] = jnp.where(row == 0, row_freq, col_freq).astype(F32).astype(BF16)
    copies[2].wait()
    copies[3].wait()
    right = jnp.zeros((TILE, TILE), F32)
    moments = jnp.concatenate([wide(0.9 * m_ref[t] + g_ref[t].astype(F32)) for t in range(4)], axis=0)
    products = fold(dot(moments, cols))
    for t in range(4):
        right = jnp.where(slot == t, products[TILE * t : TILE * t + TILE], right)
    every = fold(dot(rows, weights(right)))
    bands = jnp.zeros((BAND, TILE), F32)
    for t in range(4):
        bands = jnp.where(slot == t, every[BAND * t : BAND * t + BAND], bands)
    bands_ref[...] = bands
    packed_ref[...] = jnp.where(lane < 64, bands[:8], bands[8:])


def block_kernel(got_ref, params_ref, freq_ref, out_ref):
    first = iota((1, TILE), 1) < 64
    total = jnp.sum(got_ref[...], axis=0)
    turned = pltpu.roll(total, 64, 1)
    high, low = [p.astype(F32) for p in pieces(total)]
    turned_high, turned_low = [p.astype(F32) for p in pieces(turned)]
    bands = jnp.concatenate(
        [jnp.where(first, high, turned_low), jnp.where(first, turned_high, low)], axis=0
    ).astype(BF16)
    block = params_ref[2 * lax.axis_index("core") + lax.axis_index("yh")]
    freq = freq_ref[...]
    for d in range(16):
        out_ref[d, :128] = block
        out_ref[d, 128:144] = bands
        out_ref[d, 144:] = freq


def source(yh, s):
    return PLANE_ORDER.index(8 * yh + 4 * (s % 2) + s // 2)


def momentum_kernel(g_ref, m_ref, bands_ref, freq_ref, got_ref, down_ref, out_ref, all_rows_ref, all_cols_ref):
    lane = iota((1, TILE), 1)
    bands = bands_ref[...]
    diagonal = [jnp.where(lane // BAND == t, bands, 0.0) for t in range(4)]
    diagonal = jnp.concatenate(diagonal + [jnp.zeros((64, TILE), F32)], axis=0)
    down = down_ref[...]
    own = freq_ref[...].astype(F32).astype(jnp.int32)
    half = wide(fold(dot(jnp.concatenate(tables(own[0:1], down), axis=1), weights(diagonal))))
    cols = stacked(*tables(own[1:2], down))
    for t, mask in enumerate(masks(4, BF16)):
        moment = 0.9 * m_ref[t] + g_ref[t].astype(F32)
        out_ref[t] = moment - fold(dot_nt(half * mask, cols))
    for g in range(4):
        freqs = [got_ref[source(0, s), 144:160].astype(F32).astype(jnp.int32) for s in (2 * g, 2 * g + 1)]
        freqs = jnp.where(lane < 64, freqs[0], freqs[1])
        all_rows_ref[g] = jnp.concatenate(tables(freqs[0:1], down), axis=1)
        picks = (iota((TILE, TILE), 0) == freqs[1:2]).astype(F32).T.astype(BF16)
        both = dot_nt(picks, down)
        odd = (iota((TILE, TILE), 0) // BAND) % 2 == 1
        for sh in range(2):
            parts = []
            for part in (both[:, :TILE], both[:, TILE:]):
                spread = jnp.concatenate([jnp.where(odd, 0.0, part), jnp.where(odd, part, 0.0)], axis=1)
                parts += [spread[64 * sh : 64 * sh + 64]] * 2
            all_cols_ref[2 * g + sh] = jnp.concatenate(parts, axis=0).astype(BF16)


def update_kernel(own_ref, other_ref, rows_ref, cols_ref, out_hbm, out_ref, sems):
    lane = iota((1, TILE), 1)
    first = lane < 64
    core = lax.axis_index("core")
    halves = []
    squares = []
    for g in range(4):
        sums = []
        for s in (2 * g, 2 * g + 1):
            v = sum(ref[source(yh, s), 128:144].astype(F32) for ref in (own_ref, other_ref) for yh in range(2))
            sums.append((v + pltpu.roll(v, 64, 1)) * (1.0 / 64))
        both = jnp.where(first, sums[0], sums[1])
        squares.append(jnp.sum(both * both, axis=0, keepdims=True))
        diagonal = jnp.concatenate([jnp.where(lane // BAND == t, sums[t // 4], 0.0) for t in range(8)], axis=0)
        halves.append(fold(dot(rows_ref[g], weights(diagonal))))
    squares = jnp.concatenate(squares + squares, axis=0)
    same = (iota((TILE, TILE), 0) // BAND == iota((TILE, TILE), 1) // BAND).astype(F32).astype(BF16)
    high, low = pieces(squares)
    mean = (dot(high, same) + dot(low, same)) * (1.0 / (TILE * TILE))
    inverse = 1.0 / jnp.sqrt(mean + 1e-06)
    pair = (iota((1, 2 * TILE), 1) % 64) // (2 * BAND)
    order = ((own_ref, core), (other_ref, 1 - core))
    copies = []
    for g in range(4):
        high, low = [p.astype(F32) for p in pieces(halves[g] * inverse[g : g + 1])]
        for sh in range(2):
            s = 2 * g + sh
            if sh == 0:
                half = jnp.where(first, high, pltpu.roll(low, 64, 1)).astype(BF16)
            else:
                half = jnp.where(first, pltpu.roll(high, 64, 1), low).astype(BF16)
            half = jnp.concatenate([half, half], axis=1)
            left = jnp.concatenate([half * (pair == half_of).astype(F32).astype(BF16) for _, half_of in order], axis=0)
            update = dot(left, cols_ref[s])
            for i, (ref, half_of) in enumerate(order):
                for yh in range(2):
                    params = ref[source(yh, s), :128].astype(F32)
                    own = update[TILE * i : TILE * i + TILE, TILE * yh : TILE * yh + TILE]
                    out_ref[4 * s + 2 * half_of + yh] = (params - own).astype(BF16)
            tiles = pl.ds(4 * s, 4)
            copies.append(pltpu.make_async_copy(out_ref.at[tiles], out_hbm.at[tiles], sems.at[s]))
            copies[-1].start()
    for copy in copies:
        copy.wait()


SMEM = pl.BlockSpec(memory_space=pltpu.SMEM)
VMEM = pl.BlockSpec(memory_space=pltpu.VMEM)
HBM = pl.BlockSpec(memory_space=pltpu.HBM)
PARAMS = pltpu.CompilerParams(vmem_limit_bytes=40 * 1024 * 1024)
shape = jax.ShapeDtypeStruct


def per_device(gradients, momentum, params, band_offsets):
    down = jnp.asarray(split_table())
    g, m = gradients[0], momentum[0]
    packed, bands, freq = pl.pallas_call(
        bands_kernel,
        out_shape=(
            shape((8, TILE), F32),
            shape((BAND, TILE), F32),
            shape((BAND, TILE), BF16),
        ),
        in_specs=[HBM] * 4,
        out_specs=(VMEM,) * 3,
        scratch_shapes=[
            pltpu.SMEM((2, 4), jnp.int32),
            pltpu.VMEM((4, TILE, TILE), BF16),
            pltpu.VMEM((4, TILE, TILE), F32),
            pltpu.VMEM((2 * TILE, TILE), BF16),
            pltpu.SemaphoreType.DMA((4,)),
        ],
        compiler_params=pltpu.CompilerParams(vmem_limit_bytes=16 * 1024 * 1024),
        name="bands",
    )(*[pltpu.with_memory_space_constraint(a, pltpu.HBM) for a in (band_offsets.T, g, m, down)])
    got = lax.all_to_all(jnp.broadcast_to(packed[None], (16, 8, TILE)), "z", 0, 0, axis_index_groups=[Z_ORDER])
    blocks = pl.pallas_call(
        block_kernel,
        out_shape=shape((16, ROWS, TILE), BF16),
        in_specs=[VMEM] * 3,
        out_specs=VMEM,
        compiler_params=PARAMS,
        name="blocks",
    )(got, params, freq)
    own = lax.all_to_all(blocks, PLANE, 0, 0, axis_index_groups=[PLANE_ORDER])
    other = lax.ppermute(own, "core", [(0, 1), (1, 0)])
    new_momentum, all_rows, all_cols = pl.pallas_call(
        momentum_kernel,
        out_shape=(
            shape((4, TILE, TILE), F32),
            shape((4, TILE, 2 * TILE), BF16),
            shape((8, 2 * TILE, 2 * TILE), BF16),
        ),
        in_specs=[VMEM] * 6,
        out_specs=(VMEM,) * 3,
        compiler_params=PARAMS,
        cost_estimate=pl.CostEstimate(flops=200_000_000, bytes_accessed=700_000, transcendentals=0),
        name="momentum",
    )(g, m, bands, freq, own, down)
    whole = pl.pallas_call(
        update_kernel,
        out_shape=shape((32, TILE, TILE), BF16),
        in_specs=[VMEM] * 4,
        out_specs=HBM,
        scratch_shapes=[pltpu.VMEM((32, TILE, TILE), BF16), pltpu.SemaphoreType.DMA((8,))],
        compiler_params=PARAMS,
        name="update",
    )(own, other, all_rows, all_cols)
    return (new_momentum[None], whole)


def solution(mesh):
    fine = Mesh(mesh.devices.reshape(2, 16, 2, 4, 2), AXES)
    rep, shard = ("yh", "z", "core"), ("x", "yl")
    in_specs = (P(rep, shard, None, None), P(rep, shard, None, None), P(shard, None, None), P(shard, None))
    out_specs = (P(rep, shard, None, None), P())
    return jax.shard_map(per_device, mesh=fine, in_specs=in_specs, out_specs=out_specs, check_vma=False)
```
